32 devices in a mesh: gx: 4 (over x, core), gy: 8 (over z, y).
Axes of the slice: x: 2, y: 2, z: 4, core: 2. Of those that a mesh axis runs over, the one named last changes fastest.
Arguments:
- state: float32 [10, 32, 64, 128], P(None, 'gx', 'gy'), may hold values from 0.01 to 3, as said below
- source_in: float32 [10, 32, 64, 128], P(None, 'gx', 'gy'), may hold values from -3 to 3
- counts: int32 [32, 64], P('gx', 'gy'), may hold values from 1 to 8, as said below
- diffusivity: float32 [10], replicated, may hold values from 0.3 to 1
- log_rate: float32 [21], replicated, may hold values from 0.3 to 1
- activation: float32 [21], replicated, may hold values from 0.4 to 0.8
- heat_release: float32 [21], replicated, may hold values from -1 to 2
Outputs:
- next_state: float32 [10, 32, 64, 128], P(None, 'gx', 'gy')
- late_source: float32 [10, 32, 64, 128], P(None, 'gx', 'gy')
The draws below stay inside these ranges and needn't reach their ends.
Inputs may be any that keep to these rules, and one draw needn't show every extreme that they name: Boxes of 8 x 8 blocks are either flame boxes, about an eighth of them, where every count is 5 or more and one is 8, or others, where counts are 1 or 2. `state`: rows 0 to 8 lie in [0.01, 1]; the last row lies in [1, 3].
All inputs are finite; a program needn't handle non-finite values.
Results may differ from the reference program's by a relative error of at most 0.0003.
Values sent between devices are 32-bit elements; how exact they have to be, the bound alone decides.
A program may use at most 64 MiB of HBM per device.

```python
import math
import jax
import jax.numpy as jnp
import numpy as np
from jax import lax

SPECIES = 9
REACTIONS = 21
CMAX = 8
CX = 8
CY = 8
CZ = 128
NX = 32
NY = 64


def draw_state(key, part):
    first_key, second_key = jax.random.split(key)
    species = jax.random.uniform(first_key, (SPECIES, NX, NY, CZ), jnp.float32, 0.05, 1.0)
    temper = jax.random.uniform(second_key, (1, NX, NY, CZ), jnp.float32, 1.0, 3.0)
    return jnp.concatenate([species, temper], 0).astype(jnp.float32)


def draw_counts(key, part):
    boxes_x = NX // CX
    boxes_y = NY // CY
    perm_key, base_key, flame_key = jax.random.split(key, 3)
    ranking = jax.random.permutation(perm_key, boxes_x * boxes_y).reshape(boxes_x, boxes_y)
    flame_box = ranking < max(1, boxes_x * boxes_y // 8)
    flame = jnp.repeat(jnp.repeat(flame_box, CX, 0), CY, 1)
    base = jax.random.randint(base_key, (NX, NY), 1, 3)
    heated = jax.random.randint(flame_key, (NX, NY), 5, CMAX + 1)
    row_index = jnp.arange(NX)[:, None] % CX
    col_index = jnp.arange(NY)[None, :] % CY
    corner = (row_index == 0) & (col_index == 0)
    heated = jnp.where(corner, CMAX, heated)
    return jnp.where(flame, heated, base).astype(jnp.int32)


def shard_levels(own_key, shape, shards, smallest, high):
    loudness = 1.0
    for position, parts in shards:
        steps = jax.random.uniform(jax.random.fold_in(jax.random.fold_in(own_key, 6), position), (parts,), jnp.float32, smallest / len(shards), high / len(shards))
        loudness = loudness * jnp.repeat(jnp.exp(steps), shape[position] // parts).reshape((-1,) + (1,) * (len(shape) - 1 - position))
    return loudness


def centred(rng, dims, scale, limit, cuts=(), kind=jnp.bfloat16):
    level = shard_levels(rng, dims, cuts, -0.22, 0.18) if cuts else 1.0
    result = jax.random.normal(rng, dims, jnp.float32) * scale * level
    return jnp.minimum(jnp.maximum(result, -limit), limit).astype(kind)


def setup_inputs(seed: int = 0) -> dict:
    splits = jax.random.split(jax.random.key(seed), 8)
    state = draw_state(jax.random.fold_in(splits[7], 71), 0)
    source_in = centred(splits[1], (SPECIES + 1, NX, NY, CZ), 1.0, 3.0, ((1, 4), (2, 8)), jnp.float32)
    counts = draw_counts(jax.random.fold_in(splits[7], 71), 0)
    diffusivity = jnp.clip(jnp.exp(jax.random.uniform(splits[3], (SPECIES + 1,), jnp.float32, math.log(0.3), math.log(1.0))), 0.3, 1.0)
    log_rate = jnp.clip(jax.random.uniform(splits[4], (REACTIONS,), jnp.float32, 0.3, 1.0), 0.3, 1.0)
    activation = jnp.clip(jax.random.uniform(splits[5], (REACTIONS,), jnp.float32, 0.4, 0.8), 0.4, 0.8)
    heat_release = jnp.clip(jax.random.uniform(splits[6], (REACTIONS,), jnp.float32, -1.0, 2.0), -1.0, 2.0)
    return {"state": state, "source_in": source_in, "counts": counts, "diffusivity": diffusivity, "log_rate": log_rate, "activation": activation, "heat_release": heat_release}


time_step = 0.15

reaction_table = (
    (3, 1, (4, 5)), (4, 0, (3, 5)), (5, 0, (3, 2)), (5, 5, (4, 2)),
    (3, 3, (0,)), (3, 5, (2,)), (4, 4, (1,)), (3, 4, (5,)), (3, 1, (6,)),
    (6, 3, (0, 1)), (6, 3, (5, 5)), (6, 4, (1, 5)), (6, 5, (2, 1)),
    (6, 6, (7, 1)), (7, 9, (5, 5)), (7, 3, (2, 5)), (7, 3, (6, 0)),
    (7, 4, (5, 6)), (7, 5, (6, 2)), (0, 9, (3, 3)), (2, 9, (3, 5)),
)


def tables(heat_release):
    leading = np.zeros((21, 10), np.float32)
    trailing = np.zeros((21, 10), np.float32)
    change = np.zeros((9, 21), np.float32)
    for reaction, entry in enumerate(reaction_table):
        leading[reaction, entry[0]] = 1.0
        trailing[reaction, entry[1]] = 1.0
        change[entry[0], reaction] -= 1.0
        if entry[1] < 9:
            change[entry[1], reaction] -= 1.0
        for product in entry[2]:
            change[product, reaction] += 1.0
    matrix = jnp.concatenate([jnp.asarray(change).astype(jnp.float32), heat_release[None, :]], 0)
    return jnp.asarray(leading).astype(jnp.float32), jnp.asarray(trailing).astype(jnp.float32), matrix


def advance(current, coeffs, stride, active, leading, trailing, matrix):
    augmented = jnp.concatenate([current[:9], jnp.ones_like(current[:1])], 0)
    reactant_one = jnp.dot(leading, augmented, precision=lax.Precision.HIGHEST)
    reactant_two = jnp.dot(trailing, augmented, precision=lax.Precision.HIGHEST)
    rate_terms = coeffs * reactant_one * reactant_two
    change_now = jnp.dot(matrix, rate_terms, precision=lax.Precision.HIGHEST)
    return jnp.where(active[None, :], current + stride[None, :] * change_now, current)


def chemistry(fields_in, counts, log_rate, activation, heat_release):
    leading, trailing, matrix = tables(heat_release)

    def one_slice(pieces):
        slab, slab_counts = pieces
        cell_rows = slab.reshape(slab.shape[0], slab.shape[1] * slab.shape[2])
        counts_cells = jnp.repeat(slab_counts, slab.shape[2])
        coeffs = jnp.exp(log_rate[:, None] - activation[:, None] / cell_rows[9][None, :])
        stride = time_step / counts_cells.astype(jnp.float32)
        current = cell_rows
        for turn_index in range(CMAX):
            current = advance(current, coeffs, stride, turn_index < counts_cells, leading, trailing, matrix)
        return ((current - cell_rows) / time_step).reshape(slab.shape)

    slabs = lax.map(one_slice, (jnp.moveaxis(fields_in, 1, 0), counts))
    return jnp.moveaxis(slabs, 0, 1)


def laplace(field):
    beside = jnp.roll(field, 1, 1) + jnp.roll(field, -1, 1)
    beside = beside + jnp.roll(field, 1, 2) + jnp.roll(field, -1, 2)
    beside = beside + jnp.roll(field, 1, 3) + jnp.roll(field, -1, 3)
    return beside - 6.0 * field


def reference(state, source_in, counts, diffusivity, log_rate, activation, heat_release):
    spread = diffusivity[:, None, None, None]
    first_section = state + time_step * (spread * laplace(state) + source_in)
    early = chemistry(state, counts, log_rate, activation, heat_release)
    next_state = 0.5 * state + 0.5 * (first_section + time_step * (spread * laplace(first_section) + early))
    late_source = chemistry(first_section, counts, log_rate, activation, heat_release)
    return next_state, late_source
```

```python
import jax
import jax.numpy as jnp
import numpy as np
from jax import lax
from jax.experimental import pallas as pl
from jax.experimental.pallas import tpu as pltpu
from jax.sharding import PartitionSpec as P

time_step = 0.15
log2_e = 1.4426950408889634
most_steps = 8
rows_all = 10
reaction_table = (
    (3, 1, (4, 5)),
    (4, 0, (3, 5)),
    (5, 0, (3, 2)),
    (5, 5, (4, 2)),
    (3, 3, (0,)),
    (3, 5, (2,)),
    (4, 4, (1,)),
    (3, 4, (5,)),
    (3, 1, (6,)),
    (6, 3, (0, 1)),
    (6, 3, (5, 5)),
    (6, 4, (1, 5)),
    (6, 5, (2, 1)),
    (6, 6, (7, 1)),
    (7, 9, (5, 5)),
    (7, 3, (2, 5)),
    (7, 3, (6, 0)),
    (7, 4, (5, 6)),
    (7, 5, (6, 2)),
    (0, 9, (3, 3)),
    (2, 9, (3, 5)),
)
free_rows = (0, 1, 2, 4, 6, 7)
spanning = (7, 11, 14, 17, 19, 20)


def spanning_tables():
    change = np.zeros((9, 21))
    for reaction, (one, two, products) in enumerate(reaction_table):
        change[one, reaction] -= 1.0
        if two < 9:
            change[two, reaction] -= 1.0
        for product in products:
            change[product, reaction] += 1.0
    kept = change[list(free_rows)]
    inverse = np.round(np.linalg.inv(kept[:, list(spanning)]), 6)
    return inverse, np.round(inverse @ kept, 6)


def weighted(terms):
    total = None
    for weight, value in terms:
        if weight == 0:
            continue
        term = value if weight == 1 else value * float(weight)
        total = term if total is None else total + term
    return total


def heat_scalars(heat):
    inverse, spans = spanning_tables()
    base = [heat[r] for r in spanning]
    on_rows = [weighted([(inverse[i, j], base[i]) for i in range(6)]) for j in range(6)]
    on_reactions = {}
    for r in range(21):
        if r not in spanning:
            on_reactions[r] = weighted([(1.0, heat[r])] + [(-spans[i, r], base[i]) for i in range(6)])
    return on_rows, on_reactions


def react(u, temperature, counts, stride, log_rate, activation, heat):
    on_rows, on_reactions = heat_scalars(heat)
    inverse_t = 1.0 / temperature
    k = [jnp.exp2(log_rate[r] - activation[r] * inverse_t) * stride for r in range(21)]
    h2, o2, h2o, h, o, oh, ho2, h2o2 = u[:8]
    oxygen = 2.0 * (o2 + ho2 + h2o2) + h2o + o + oh
    surplus = 2.0 * (h2 - o2) + h2o + h - ho2 - o
    sums = None
    for step in range(most_steps):
        if step == 0:
            a, b, c, d, e, f, g, i = h2, h2o, h, o, oh, ho2, h2o2, o2
        else:
            active = counts > float(step)
            a, b, c, d, e, f, g = [jnp.where(active, v, 0.0) for v in (h2, h2o, h, o, oh, ho2, h2o2)]
            i = o2
        p = {0: c * i, 1: d * a, 2: e * a, 3: e * e, 4: c * c, 5: c * e, 6: d * d, 9: f * c, 12: f * e, 13: f * f,
             15: g * c, 18: g * e}
        w = {r: k[r] * v for r, v in p.items()}
        w[8] = k[8] * p[0]
        w[10] = k[10] * p[9]
        w[16] = k[16] * p[15]
        w[7] = k[7] * (c * d)
        w[11] = k[11] * (f * d)
        w[17] = k[17] * (g * d)
        w[14] = k[14] * g
        w[19] = k[19] * a
        w[20] = k[20] * b
        s1 = w[16] + w[17] + w[18]
        s2 = (w[9] + w[13]) + (w[11] + w[12])
        h2 = h2 + (((w[4] + w[9]) + (w[16] - w[1])) - (w[2] + w[19]))
        o2 = o2 + ((s2 + w[6]) - (w[0] + w[8]))
        h2o = h2o + (((w[2] + w[3]) + (w[5] + w[12])) + ((w[15] + w[18]) - w[20]))
        o = o + (((w[0] + w[3]) - (w[1] + w[7])) - ((w[6] + w[6]) + (w[11] + w[17])))
        ho2 = ho2 + (((s1 + w[8]) - s2) - (w[10] + w[13]))
        h2o2 = h2o2 + ((w[13] - s1) - (w[14] + w[15]))
        oh = ((oxygen - h2o) - o) - 2.0 * ((o2 + ho2) + h2o2)
        h = ((surplus - h2o) + (ho2 + o)) - 2.0 * (h2 - o2)
        sums = p if sums is None else {r: sums[r] + p[r] for r in sums}
    now = (h2, o2, h2o, h, o, oh, ho2, h2o2)
    change = [after - before for after, before in zip(now, u[:8])]
    rate = {r: on_reactions[r] * k[r] for r in on_reactions}
    rate[0] = rate[0] + rate.pop(8)
    rate[9] = rate[9] + rate.pop(10)
    rate[15] = rate[15] + rate.pop(16)
    warm = None
    for r, total in sums.items():
        term = rate[r] * total
        warm = term if warm is None else warm + term
    for weight, row in zip(on_rows, free_rows):
        warm = warm + weight * change[row]
    return change + [jnp.zeros_like(warm), warm]


def kernel(
    state, source, counts, diffusivity, log_rate, activation, heat,
    next_out, late_out,
    st, src, first, q, late, nxt, steps, strides, rates,
    hx1, hy1, hx2, hy2,
    load_sem, late_sem, next_sem, send_sem, recv_sem,
):
    rows, nx, ny, nz = st.shape
    loads = [
        pltpu.make_async_copy(state, st, load_sem.at[0]),
        pltpu.make_async_copy(source, src, load_sem.at[1]),
    ]
    for load in loads:
        load.start()

    x, size_x = lax.axis_index("gx"), lax.axis_size("gx")
    y, size_y = lax.axis_index("gy"), lax.axis_size("gy")
    neighbours = (
        {"gx": lax.rem(x + 1, size_x)},
        {"gx": lax.rem(x + size_x - 1, size_x)},
        {"gy": lax.rem(y + 1, size_y)},
        {"gy": lax.rem(y + size_y - 1, size_y)},
    )
    barrier = pltpu.get_barrier_semaphore()
    for device in neighbours:
        pl.semaphore_signal(barrier, inc=1, device_id=device, device_id_type=pl.DeviceIdType.MESH)
    pl.semaphore_wait(barrier, 4)

    def exchange(field, halo_x, halo_y, turn):
        pieces = (
            (field.at[:, nx - 1], halo_x.at[0]),
            (field.at[:, 0], halo_x.at[1]),
            (field.at[:, :, ny - 1], halo_y.at[0]),
            (field.at[:, :, 0], halo_y.at[1]),
        )
        copies = []
        for place, (piece, device) in enumerate(zip(pieces, neighbours)):
            copies.append(pltpu.make_async_remote_copy(
                src_ref=piece[0], dst_ref=piece[1],
                send_sem=send_sem.at[turn, place], recv_sem=recv_sem.at[turn, place],
                device_id=device, device_id_type=pl.DeviceIdType.MESH,
            ))
        for copy in copies:
            copy.start()
        return copies

    first_copies = exchange(state, hx1, hy1, 0)

    for r in range(21):
        rates[0, r] = log_rate[r] * log2_e
        rates[1, r] = activation[r] * log2_e
    row_index = lax.broadcasted_iota(jnp.int32, (ny, nz), 0)
    for i in range(nx):
        number = jnp.zeros((ny, nz), jnp.int32)
        for j in range(ny):
            number = jnp.where(row_index == j, counts[i, j], number)
        number = number.astype(jnp.float32)
        steps[i] = number
        strides[i] = time_step / number

    def chemistry(field, i):
        u = [field[s, i] for s in range(rows)]
        return u, react(
            u, u[9], steps[i], strides[i], [rates[0, r] for r in range(21)], [rates[1, r] for r in range(21)], heat,
        )

    def laplace(field, halo_x, halo_y, k, i):
        here = field[k, i]
        before = halo_x[0, k] if i == 0 else field[k, i - 1]
        after = halo_x[1, k] if i == nx - 1 else field[k, i + 1]
        low = jnp.where(row_index == 0, halo_y[0, k, pl.ds(i, 1), :], pltpu.roll(here, 1, 0))
        high = jnp.where(row_index == ny - 1, halo_y[1, k, pl.ds(i, 1), :], pltpu.roll(here, ny - 1, 0))
        beside = (before + after) + (low + high) + (pltpu.roll(here, 1, 1) + pltpu.roll(here, nz - 1, 1))
        return beside - 6.0 * here

    loads[0].wait()

    def early_group(i, carry):
        u, change = chemistry(st, i)
        for s in range(rows):
            q[s, i] = u[s] + change[s]
        return carry

    lax.fori_loop(0, nx, early_group, 0)

    loads[1].wait()
    for copy in first_copies:
        copy.wait()

    def first_row(k, carry):
        spread = diffusivity[k]
        for i in range(nx):
            value = st[k, i] + time_step * (spread * laplace(st, hx1, hy1, k, i) + src[k, i])
            first[k, i] = value
            q[k, i] = q[k, i] + value
        return carry

    lax.fori_loop(0, rows, first_row, 0)
    second_copies = exchange(first, hx2, hy2, 1)

    def late_copy(i):
        return pltpu.make_async_copy(late.at[:, i], late_out.at[:, i], late_sem.at[i])

    def late_group(i, carry):
        u, change = chemistry(first, i)
        for s in range(rows):
            late[s, i] = change[s] * (1.0 / time_step)
        late_copy(i).start()
        return carry

    half = nx // 2
    lax.fori_loop(0, half, late_group, 0)
    for copy in second_copies:
        copy.wait()

    def next_row(k, carry):
        weight = (0.5 * time_step) * diffusivity[k]
        for i in range(nx):
            nxt[k, i] = 0.5 * q[k, i] + weight * laplace(first, hx2, hy2, k, i)
        return carry

    lax.fori_loop(0, rows, next_row, 0)
    next_copy = pltpu.make_async_copy(nxt, next_out, next_sem)
    next_copy.start()
    lax.fori_loop(half, nx, late_group, 0)

    next_copy.wait()
    for i in range(nx):
        late_copy(i).wait()


def local(state, source_in, counts, diffusivity, log_rate, activation, heat_release):
    rows, nx, ny, nz = state.shape
    whole = (rows, nx, ny, nz)
    field = pltpu.VMEM(whole, jnp.float32)
    anywhere = pl.BlockSpec(memory_space=pl.ANY)
    scalars = pl.BlockSpec(memory_space=pltpu.SMEM)
    return pl.pallas_call(
        kernel,
        out_shape=(jax.ShapeDtypeStruct(whole, jnp.float32),) * 2,
        in_specs=[anywhere, anywhere, scalars, scalars, scalars, scalars, scalars],
        out_specs=(anywhere, anywhere),
        scratch_shapes=[
            field, field, field, field, field, field,
            pltpu.VMEM((nx, ny, nz), jnp.float32),
            pltpu.VMEM((nx, ny, nz), jnp.float32),
            pltpu.SMEM((2, 21), jnp.float32),
            pltpu.VMEM((2, rows, ny, nz), jnp.float32),
            pltpu.VMEM((2, rows, nx, nz), jnp.float32),
            pltpu.VMEM((2, rows, ny, nz), jnp.float32),
            pltpu.VMEM((2, rows, nx, nz), jnp.float32),
            pltpu.SemaphoreType.DMA((2,)),
            pltpu.SemaphoreType.DMA((nx,)),
            pltpu.SemaphoreType.DMA,
            pltpu.SemaphoreType.DMA((2, 4)),
            pltpu.SemaphoreType.DMA((2, 4)),
        ],
        compiler_params=pltpu.CompilerParams(
            collective_id=0, has_side_effects=True, vmem_limit_bytes=32 * 1024 * 1024,
        ),
        name="jet",
    )(state, source_in, counts, diffusivity, log_rate, activation, heat_release)


def solution(mesh):
    grid = P(None, "gx", "gy", None)
    return jax.shard_map(
        local,
        mesh=mesh,
        in_specs=(grid, grid, P("gx", "gy"), P(), P(), P(), P()),
        out_specs=(grid, grid),
        check_vma=False,
    )
```

```python
import jax
import jax.numpy as jnp
import numpy as np
from jax import lax
from jax.experimental import pallas as pl
from jax.experimental.pallas import tpu as pltpu
from jax.sharding import PartitionSpec as P

time_step = 0.15
log2_e = 1.4426950408889634
most_steps = 8
together = 2
reaction_table = (
    (3, 1, (4, 5)),
    (4, 0, (3, 5)),
    (5, 0, (3, 2)),
    (5, 5, (4, 2)),
    (3, 3, (0,)),
    (3, 5, (2,)),
    (4, 4, (1,)),
    (3, 4, (5,)),
    (3, 1, (6,)),
    (6, 3, (0, 1)),
    (6, 3, (5, 5)),
    (6, 4, (1, 5)),
    (6, 5, (2, 1)),
    (6, 6, (7, 1)),
    (7, 9, (5, 5)),
    (7, 3, (2, 5)),
    (7, 3, (6, 0)),
    (7, 4, (5, 6)),
    (7, 5, (6, 2)),
    (0, 9, (3, 3)),
    (2, 9, (3, 5)),
)
free_rows = (0, 1, 2, 4, 6, 7)
spanning = (7, 11, 14, 17, 19, 20)


def spanning_tables():
    change = np.zeros((9, 21))
    for reaction, (one, two, products) in enumerate(reaction_table):
        change[one, reaction] -= 1.0
        if two < 9:
            change[two, reaction] -= 1.0
        for product in products:
            change[product, reaction] += 1.0
    kept = change[list(free_rows)]
    inverse = np.round(np.linalg.inv(kept[:, list(spanning)]), 6)
    return inverse, np.round(inverse @ kept, 6)


def weighted(terms):
    total = None
    for weight, value in terms:
        if weight == 0:
            continue
        term = value if weight == 1 else value * float(weight)
        total = term if total is None else total + term
    return total


def heat_scalars(heat):
    inverse, spans = spanning_tables()
    base = [heat[r] for r in spanning]
    on_rows = [weighted([(inverse[i, j], base[i]) for i in range(6)]) for j in range(6)]
    on_reactions = {}
    for r in range(21):
        if r not in spanning:
            on_reactions[r] = weighted([(1.0, heat[r])] + [(-spans[i, r], base[i]) for i in range(6)])
    return on_rows, on_reactions


def react(u, temperature, counts, stride, log_rate, activation, heat):
    on_rows, on_reactions = heat_scalars(heat)
    inverse_t = 1.0 / temperature
    k = [jnp.exp2(log_rate[r] - activation[r] * inverse_t) * stride for r in range(21)]
    h2, o2, h2o, h, o, oh, ho2, h2o2 = u[:8]
    oxygen = 2.0 * (o2 + ho2 + h2o2) + h2o + o + oh
    surplus = 2.0 * (h2 - o2) + h2o + h - ho2 - o
    sums = None
    for step in range(most_steps):
        if step == 0:
            a, b, c, d, e, f, g, i = h2, h2o, h, o, oh, ho2, h2o2, o2
        else:
            active = counts > float(step)
            a, b, c, d, e, f, g = [jnp.where(active, v, 0.0) for v in (h2, h2o, h, o, oh, ho2, h2o2)]
            i = o2
        p = {0: c * i, 1: d * a, 2: e * a, 3: e * e, 4: c * c, 5: c * e, 6: d * d, 9: f * c, 12: f * e, 13: f * f,
             15: g * c, 18: g * e}
        w = {r: k[r] * v for r, v in p.items()}
        w[8] = k[8] * p[0]
        w[10] = k[10] * p[9]
        w[16] = k[16] * p[15]
        w[7] = k[7] * (c * d)
        w[11] = k[11] * (f * d)
        w[17] = k[17] * (g * d)
        w[14] = k[14] * g
        w[19] = k[19] * a
        w[20] = k[20] * b
        s1 = w[16] + w[17] + w[18]
        s2 = (w[9] + w[13]) + (w[11] + w[12])
        h2 = h2 + (((w[4] + w[9]) + (w[16] - w[1])) - (w[2] + w[19]))
        o2 = o2 + ((s2 + w[6]) - (w[0] + w[8]))
        h2o = h2o + (((w[2] + w[3]) + (w[5] + w[12])) + ((w[15] + w[18]) - w[20]))
        o = o + (((w[0] + w[3]) - (w[1] + w[7])) - ((w[6] + w[6]) + (w[11] + w[17])))
        ho2 = ho2 + (((s1 + w[8]) - s2) - (w[10] + w[13]))
        h2o2 = h2o2 + ((w[13] - s1) - (w[14] + w[15]))
        oh = ((oxygen - h2o) - o) - 2.0 * ((o2 + ho2) + h2o2)
        h = ((surplus - h2o) + (ho2 + o)) - 2.0 * (h2 - o2)
        sums = p if sums is None else {r: sums[r] + p[r] for r in sums}
    now = (h2, o2, h2o, h, o, oh, ho2, h2o2)
    change = [after - before for after, before in zip(now, u[:8])]
    rate = {r: on_reactions[r] * k[r] for r in on_reactions}
    rate[0] = rate[0] + rate.pop(8)
    rate[9] = rate[9] + rate.pop(10)
    rate[15] = rate[15] + rate.pop(16)
    warm = None
    for r, total in sums.items():
        term = rate[r] * total
        warm = term if warm is None else warm + term
    for weight, row in zip(on_rows, free_rows):
        warm = warm + weight * change[row]
    return change + [jnp.zeros_like(warm), warm]


def kernel(
    state, source, counts, diffusivity, log_rate, activation, heat,
    next_out, late_out,
    st, src, first, q, late, nxt, steps, strides, rates,
    hx1, hy1, hx2, hy2,
    load_sem, late_sem, next_sem, send_sem, recv_sem,
):
    rows, nx, ny, nz = st.shape
    groups = nx // together
    loads = [
        pltpu.make_async_copy(state, st, load_sem.at[0]),
        pltpu.make_async_copy(source, src, load_sem.at[1]),
    ]
    for load in loads:
        load.start()

    x, size_x = lax.axis_index("gx"), lax.axis_size("gx")
    y, size_y = lax.axis_index("gy"), lax.axis_size("gy")
    neighbours = (
        {"gx": lax.rem(x + 1, size_x)},
        {"gx": lax.rem(x + size_x - 1, size_x)},
        {"gy": lax.rem(y + 1, size_y)},
        {"gy": lax.rem(y + size_y - 1, size_y)},
    )
    barrier = pltpu.get_barrier_semaphore()
    for device in neighbours:
        pl.semaphore_signal(barrier, inc=1, device_id=device, device_id_type=pl.DeviceIdType.MESH)
    pl.semaphore_wait(barrier, 4)

    def exchange(field, halo_x, halo_y, turn):
        pieces = (
            (field.at[:, nx - 1], halo_x.at[0]),
            (field.at[:, 0], halo_x.at[1]),
            (field.at[:, :, ny - 1], halo_y.at[0]),
            (field.at[:, :, 0], halo_y.at[1]),
        )
        copies = []
        for place, (piece, device) in enumerate(zip(pieces, neighbours)):
            copies.append(pltpu.make_async_remote_copy(
                src_ref=piece[0], dst_ref=piece[1],
                send_sem=send_sem.at[turn, place], recv_sem=recv_sem.at[turn, place],
                device_id=device, device_id_type=pl.DeviceIdType.MESH,
            ))
        for copy in copies:
            copy.start()
        return copies

    first_copies = exchange(state, hx1, hy1, 0)

    for r in range(21):
        rates[0, r] = log_rate[r] * log2_e
        rates[1, r] = activation[r] * log2_e
    row_index = lax.broadcasted_iota(jnp.int32, (ny, nz), 0)
    for i in range(nx):
        number = jnp.zeros((ny, nz), jnp.int32)
        for j in range(ny):
            number = jnp.where(row_index == j, counts[i, j], number)
        number = number.astype(jnp.float32)
        steps[i] = number
        strides[i] = time_step / number

    def chemistry(field, i):
        part = pl.ds(i * together, together)
        u = [field[s, part] for s in range(rows)]
        return u, react(
            u, u[9], steps[part], strides[part], [rates[0, r] for r in range(21)], [rates[1, r] for r in range(21)], heat,
        )

    def laplace(field, halo_x, halo_y, k, i):
        here = field[k, i]
        before = halo_x[0, k] if i == 0 else field[k, i - 1]
        after = halo_x[1, k] if i == nx - 1 else field[k, i + 1]
        low = jnp.where(row_index == 0, halo_y[0, k, pl.ds(i, 1), :], pltpu.roll(here, 1, 0))
        high = jnp.where(row_index == ny - 1, halo_y[1, k, pl.ds(i, 1), :], pltpu.roll(here, ny - 1, 0))
        beside = (before + after) + (low + high) + (pltpu.roll(here, 1, 1) + pltpu.roll(here, nz - 1, 1))
        return beside - 6.0 * here

    loads[0].wait()

    def early_group(i, carry):
        u, change = chemistry(st, i)
        for s in range(rows):
            q[s, pl.ds(i * together, together)] = u[s] + change[s]
        return carry

    lax.fori_loop(0, groups, early_group, 0)

    loads[1].wait()
    for copy in first_copies:
        copy.wait()

    def first_row(k, carry):
        spread = diffusivity[k]
        for i in range(nx):
            value = st[k, i] + time_step * (spread * laplace(st, hx1, hy1, k, i) + src[k, i])
            first[k, i] = value
            q[k, i] = q[k, i] + value
        return carry

    lax.fori_loop(0, rows, first_row, 0)
    second_copies = exchange(first, hx2, hy2, 1)

    def late_copy(i):
        part = pl.ds(i * together, together)
        return pltpu.make_async_copy(late.at[:, part], late_out.at[:, part], late_sem.at[i])

    def late_group(i, carry):
        u, change = chemistry(first, i)
        for s in range(rows):
            late[s, pl.ds(i * together, together)] = change[s] * (1.0 / time_step)
        late_copy(i).start()
        return carry

    half = groups // 2
    lax.fori_loop(0, half, late_group, 0)
    for copy in second_copies:
        copy.wait()

    def next_row(k, carry):
        weight = (0.5 * time_step) * diffusivity[k]
        for i in range(nx):
            nxt[k, i] = 0.5 * q[k, i] + weight * laplace(first, hx2, hy2, k, i)
        return carry

    lax.fori_loop(0, rows, next_row, 0)
    next_copy = pltpu.make_async_copy(nxt, next_out, next_sem)
    next_copy.start()
    lax.fori_loop(half, groups, late_group, 0)

    next_copy.wait()
    for i in range(groups):
        late_copy(i).wait()


def local(state, source_in, counts, diffusivity, log_rate, activation, heat_release):
    rows, nx, ny, nz = state.shape
    whole = (rows, nx, ny, nz)
    field = pltpu.VMEM(whole, jnp.float32)
    anywhere = pl.BlockSpec(memory_space=pl.ANY)
    scalars = pl.BlockSpec(memory_space=pltpu.SMEM)
    return pl.pallas_call(
        kernel,
        out_shape=(jax.ShapeDtypeStruct(whole, jnp.float32),) * 2,
        in_specs=[anywhere, anywhere, scalars, scalars, scalars, scalars, scalars],
        out_specs=(anywhere, anywhere),
        scratch_shapes=[
            field, field, field, field, field, field,
            pltpu.VMEM((nx, ny, nz), jnp.float32),
            pltpu.VMEM((nx, ny, nz), jnp.float32),
            pltpu.SMEM((2, 21), jnp.float32),
            pltpu.VMEM((2, rows, ny, nz), jnp.float32),
            pltpu.VMEM((2, rows, nx, nz), jnp.float32),
            pltpu.VMEM((2, rows, ny, nz), jnp.float32),
            pltpu.VMEM((2, rows, nx, nz), jnp.float32),
            pltpu.SemaphoreType.DMA((2,)),
            pltpu.SemaphoreType.DMA((nx,)),
            pltpu.SemaphoreType.DMA,
            pltpu.SemaphoreType.DMA((2, 4)),
            pltpu.SemaphoreType.DMA((2, 4)),
        ],
        compiler_params=pltpu.CompilerParams(
            collective_id=0, has_side_effects=True, vmem_limit_bytes=60 * 1024 * 1024,
        ),
        name="jet",
    )(state, source_in, counts, diffusivity, log_rate, activation, heat_release)


def solution(mesh):
    grid = P(None, "gx", "gy", None)
    return jax.shard_map(
        local,
        mesh=mesh,
        in_specs=(grid, grid, P("gx", "gy"), P(), P(), P(), P()),
        out_specs=(grid, grid),
        check_vma=False,
    )
```

```python
import jax
import jax.numpy as jnp
import numpy as np
from jax import lax
from jax.experimental import pallas as pl
from jax.experimental.pallas import tpu as pltpu
from jax.sharding import PartitionSpec as P

time_step = 0.15
log2_e = 1.4426950408889634
early_steps = 2
reaction_table = (
    (3, 1, (4, 5)),
    (4, 0, (3, 5)),
    (5, 0, (3, 2)),
    (5, 5, (4, 2)),
    (3, 3, (0,)),
    (3, 5, (2,)),
    (4, 4, (1,)),
    (3, 4, (5,)),
    (3, 1, (6,)),
    (6, 3, (0, 1)),
    (6, 3, (5, 5)),
    (6, 4, (1, 5)),
    (6, 5, (2, 1)),
    (6, 6, (7, 1)),
    (7, 9, (5, 5)),
    (7, 3, (2, 5)),
    (7, 3, (6, 0)),
    (7, 4, (5, 6)),
    (7, 5, (6, 2)),
    (0, 9, (3, 3)),
    (2, 9, (3, 5)),
)
free_rows = (0, 1, 2, 4, 6, 7)
spanning = (7, 11, 14, 17, 19, 20)


def spanning_tables():
    change = np.zeros((9, 21))
    for reaction, (one, two, products) in enumerate(reaction_table):
        change[one, reaction] -= 1.0
        if two < 9:
            change[two, reaction] -= 1.0
        for product in products:
            change[product, reaction] += 1.0
    kept = change[list(free_rows)]
    inverse = np.round(np.linalg.inv(kept[:, list(spanning)]), 6)
    return inverse, np.round(inverse @ kept, 6)


def weighted(terms):
    total = None
    for weight, value in terms:
        if weight == 0:
            continue
        term = value if weight == 1 else value * float(weight)
        total = term if total is None else total + term
    return total


def heat_scalars(heat):
    inverse, spans = spanning_tables()
    base = [heat[r] for r in spanning]
    on_rows = [weighted([(inverse[i, j], base[i]) for i in range(6)]) for j in range(6)]
    on_reactions = {}
    for r in range(21):
        if r not in spanning:
            on_reactions[r] = weighted([(1.0, heat[r])] + [(-spans[i, r], base[i]) for i in range(6)])
    return on_rows, on_reactions


def prepare(temperature, stride, log_rate, activation):
    inverse_t = 1.0 / temperature
    return [jnp.exp2(log_rate[r] * log2_e - (activation[r] * log2_e) * inverse_t) * stride for r in range(21)]


def atoms(u):
    h2, o2, h2o, h, o, oh, ho2, h2o2 = u
    oxygen = 2.0 * (o2 + ho2 + h2o2) + h2o + o + oh
    surplus = 2.0 * (h2 - o2) + h2o + h - ho2 - o
    return oxygen, surplus


def substep(u, kept, k, active):
    h2, o2, h2o, h, o, oh, ho2, h2o2 = u
    oxygen, surplus = kept
    a, b, c, d, e, f, g = (h2, h2o, h, o, oh, ho2, h2o2)
    if active is not None:
        a, b, c, d, e, f, g = [jnp.where(active, v, 0.0) for v in (a, b, c, d, e, f, g)]
    p = {0: c * o2, 1: d * a, 2: e * a, 3: e * e, 4: c * c, 5: c * e, 6: d * d, 9: f * c, 12: f * e, 13: f * f,
         15: g * c, 18: g * e}
    w = {r: k[r] * v for r, v in p.items()}
    w[8] = k[8] * p[0]
    w[10] = k[10] * p[9]
    w[16] = k[16] * p[15]
    w[7] = k[7] * (c * d)
    w[11] = k[11] * (f * d)
    w[17] = k[17] * (g * d)
    w[14] = k[14] * g
    w[19] = k[19] * a
    w[20] = k[20] * b
    s1 = w[16] + w[17] + w[18]
    s2 = (w[9] + w[13]) + (w[11] + w[12])
    h2 = h2 + (((w[4] + w[9]) + (w[16] - w[1])) - (w[2] + w[19]))
    o2 = o2 + ((s2 + w[6]) - (w[0] + w[8]))
    h2o = h2o + (((w[2] + w[3]) + (w[5] + w[12])) + ((w[15] + w[18]) - w[20]))
    o = o + (((w[0] + w[3]) - (w[1] + w[7])) - ((w[6] + w[6]) + (w[11] + w[17])))
    ho2 = ho2 + (((s1 + w[8]) - s2) - (w[10] + w[13]))
    h2o2 = h2o2 + ((w[13] - s1) - (w[14] + w[15]))
    oh = ((oxygen - h2o) - o) - 2.0 * ((o2 + ho2) + h2o2)
    h = ((surplus - h2o) + (ho2 + o)) - 2.0 * (h2 - o2)
    return (h2, o2, h2o, h, o, oh, ho2, h2o2), p


def warmth(change, sums, k, heat):
    on_rows, on_reactions = heat_scalars(heat)
    rate = {r: on_reactions[r] * k[r] for r in on_reactions}
    rate[0] = rate[0] + rate.pop(8)
    rate[9] = rate[9] + rate.pop(10)
    rate[15] = rate[15] + rate.pop(16)
    terms = [rate[r] * total for r, total in sums.items()]
    terms += [weight * change[row] for weight, row in zip(on_rows, free_rows)]
    while len(terms) > 1:
        terms = [sum(terms[i + 1:i + 2], terms[i]) for i in range(0, len(terms), 2)]
    return terms[0]


def begin_chemistry(u, counts, stride, log_rate, activation, heat):
    k = prepare(u[9], stride, log_rate, activation)
    before = tuple(u[:8])
    kept = atoms(before)
    now, sums = substep(before, kept, k, None)
    for turn in range(1, early_steps):
        now, p = substep(now, kept, k, counts > float(turn))
        sums = {r: sums[r] + p[r] for r in sums}
    change = [after - start for after, start in zip(now, before)]
    return change + [jnp.zeros_like(u[9]), warmth(change, sums, k, heat)]


def finish_chemistry(parts, counts, stride, last, log_rate, activation, heat):
    number = len(parts)
    ks = [prepare(u[9], stride, log_rate, activation) for u, _ in parts]
    starts = [tuple(a + b for a, b in zip(u[:8], change[:8])) for u, change in parts]
    kept = [atoms(start) for start in starts]
    names = (0, 1, 2, 3, 4, 5, 6, 9, 12, 13, 15, 18)
    zero = jnp.zeros_like(counts)

    def turn(index, carry):
        active = counts > index.astype(jnp.float32)
        result = []
        for n in range(number):
            now, sums = carry[n]
            now, p = substep(now, kept[n], ks[n], active)
            result.append((now, tuple(total + p[r] for r, total in zip(names, sums))))
        return tuple(result)

    ends = lax.fori_loop(early_steps, last, turn, tuple((start, (zero,) * len(names)) for start in starts))
    results = []
    for n in range(number):
        now, sums = ends[n]
        more = [after - start for after, start in zip(now, starts[n])]
        warm = warmth(more, dict(zip(names, sums)), ks[n], heat)
        results.append(more + [zero, warm])
    return results


def block_numbers(counts, i, row_index, ny):
    number = jnp.zeros(row_index.shape, jnp.int32)
    for j in range(ny):
        number = jnp.where(row_index == j, counts[i, j], number)
    return number.astype(jnp.float32)


def first_kernel(
    state, source, counts_in, diffusivity_in, log_rate_in, activation_in, heat_in,
    first_out, early_out, late_out, next_out,
    st, src, first, early, late, nxt, counts, diffusivity, log_rate, activation, heat,
    hx1, hy1, hx2, hy2,
    load_sem, store_sem, send_sem, recv_sem,
):
    rows, nx, ny, nz = st.shape
    x, size_x = lax.axis_index("gx"), lax.axis_size("gx")
    y, size_y = lax.axis_index("gy"), lax.axis_size("gy")
    neighbours = (
        {"gx": lax.rem(x + 1, size_x)},
        {"gx": lax.rem(x + size_x - 1, size_x)},
        {"gy": lax.rem(y + 1, size_y)},
        {"gy": lax.rem(y + size_y - 1, size_y)},
    )
    barrier = pltpu.get_barrier_semaphore()
    for device in neighbours:
        pl.semaphore_signal(barrier, inc=1, device_id=device, device_id_type=pl.DeviceIdType.MESH)
    pairs = (
        (state, st), (counts_in, counts), (log_rate_in, log_rate), (activation_in, activation), (heat_in, heat),
        (diffusivity_in, diffusivity), (source, src),
    )
    loads = [pltpu.make_async_copy(one, two, load_sem.at[n]) for n, (one, two) in enumerate(pairs)]
    for load in loads:
        load.start()
    pl.semaphore_wait(barrier, 4)

    def exchange(field, halo_x, halo_y, turn):
        pieces = (
            (field.at[:, nx - 1], halo_x.at[0]),
            (field.at[:, 0], halo_x.at[1]),
            (field.at[:, :, ny - 1], halo_y.at[0]),
            (field.at[:, :, 0], halo_y.at[1]),
        )
        copies = []
        for place, (piece, device) in enumerate(zip(pieces, neighbours)):
            copies.append(pltpu.make_async_remote_copy(
                src_ref=piece[0], dst_ref=piece[1],
                send_sem=send_sem.at[turn, place], recv_sem=recv_sem.at[turn, place],
                device_id=device, device_id_type=pl.DeviceIdType.MESH,
            ))
        for place in (2, 3, 0, 1):
            copies[place].start()
        return copies

    first_copies = exchange(state, hx1, hy1, 0)
    row_index = lax.broadcasted_iota(jnp.int32, (ny, nz), 0)

    def laplace(field, halo_x, halo_y, k, i):
        here = field[k, i]
        before = halo_x[0, k] if i == 0 else field[k, i - 1]
        after = halo_x[1, k] if i == nx - 1 else field[k, i + 1]
        low = jnp.where(row_index == 0, halo_y[0, k, pl.ds(i, 1), :], pltpu.roll(here, 1, 0))
        high = jnp.where(row_index == ny - 1, halo_y[1, k, pl.ds(i, 1), :], pltpu.roll(here, ny - 1, 0))
        beside = (before + after) + (low + high) + (pltpu.roll(here, 1, 1) + pltpu.roll(here, nz - 1, 1))
        return beside - 6.0 * here

    def chemistry(field, into, scale=None):
        def group(i, carry):
            u = [field[s, i] for s in range(rows)]
            number = block_numbers(counts, i, row_index, ny)
            change = begin_chemistry(u, number, time_step / number, log_rate, activation, heat)
            for s in range(rows):
                into[s, i] = change[s] if scale is None else scale * change[s]
            return carry

        lax.fori_loop(0, nx, group, 0)

    for load in loads:
        load.wait()
    stores = [
        pltpu.make_async_copy(one, two, store_sem.at[n])
        for n, (one, two) in enumerate(((early, early_out), (first, first_out), (late, late_out), (nxt, next_out)))
    ]
    chemistry(st, early)
    stores[0].start()
    for copy in first_copies:
        copy.wait()

    def first_row(k, carry):
        spread = diffusivity[k]
        for i in range(nx):
            first[k, i] = st[k, i] + time_step * (spread * laplace(st, hx1, hy1, k, i) + src[k, i])
        return carry

    lax.fori_loop(0, rows, first_row, 0)
    second_copies = exchange(first, hx2, hy2, 1)
    stores[1].start()
    chemistry(first, late, 1.0 / time_step)
    stores[2].start()
    for copy in second_copies:
        copy.wait()

    def next_row(k, carry):
        weight = (0.5 * time_step) * diffusivity[k]
        for i in range(nx):
            held = 0.5 * ((st[k, i] + first[k, i]) + early[k, i])
            nxt[k, i] = held + weight * laplace(first, hx2, hy2, k, i)
        return carry

    lax.fori_loop(0, rows, next_row, 0)
    stores[3].start()
    for store in stores:
        store.wait()


def second_kernel(
    state, first_in, early_in, late_in, next_in, counts_in, log_rate_in, activation_in, heat_in,
    next_out, late_out,
    st, first, early, late, nxt, counts, log_rate, activation, heat, load_sem, next_sem, late_sem,
):
    rows, nx, ny, nz = st.shape
    pairs = (
        (counts_in, counts), (log_rate_in, log_rate), (activation_in, activation), (heat_in, heat),
        (next_in, nxt), (late_in, late), (state, st), (first_in, first), (early_in, early),
    )
    loads = [pltpu.make_async_copy(one, two, load_sem.at[n]) for n, (one, two) in enumerate(pairs)]
    for load in loads:
        load.start()
    for load in loads:
        load.wait()
    row_index = lax.broadcasted_iota(jnp.int32, (ny, nz), 0)

    def out_copies(i):
        return (
            pltpu.make_async_copy(nxt.at[:, i], next_out.at[:, i], next_sem.at[i]),
            pltpu.make_async_copy(late.at[:, i], late_out.at[:, i], late_sem.at[i]),
        )

    def group(i, carry):
        last = counts[i, 0]
        for j in range(1, ny):
            last = jnp.maximum(last, counts[i, j])

        @pl.when(last > early_steps)
        def _():
            number = block_numbers(counts, i, row_index, ny)
            fields = ([st[s, i] for s in range(rows)], [first[s, i] for s in range(rows)])
            changes = ([early[s, i] for s in range(rows)], [late[s, i] * time_step for s in range(rows)])
            early_more, late_more = finish_chemistry(
                tuple(zip(fields, changes)), number, time_step / number, last, log_rate, activation, heat,
            )
            for s in range(rows):
                nxt[s, i] = nxt[s, i] + 0.5 * early_more[s]
                late[s, i] = late[s, i] + late_more[s] * (1.0 / time_step)

        for copy in out_copies(i):
            copy.start()
        return carry

    lax.fori_loop(0, nx, group, 0)
    for i in range(nx):
        for copy in out_copies(i):
            copy.wait()


def local(state, source_in, counts, diffusivity, log_rate, activation, heat_release):
    rows, nx, ny, nz = state.shape
    whole = jax.ShapeDtypeStruct(state.shape, jnp.float32)
    field = pltpu.VMEM(state.shape, jnp.float32)
    outside = pl.BlockSpec(memory_space=pl.ANY)
    scalars = [pltpu.SMEM(a.shape, a.dtype) for a in (counts, log_rate, activation, heat_release)]
    halo_x = pltpu.VMEM((2, rows, ny, nz), jnp.float32)
    halo_y = pltpu.VMEM((2, rows, nx, nz), jnp.float32)
    first, early, late, partial = pl.pallas_call(
        first_kernel,
        out_shape=(whole,) * 4,
        in_specs=[outside] * 7,
        out_specs=(outside,) * 4,
        scratch_shapes=[
            field, field, field, field, field, field,
            scalars[0], pltpu.SMEM(diffusivity.shape, jnp.float32), *scalars[1:],
            halo_x, halo_y, halo_x, halo_y,
            pltpu.SemaphoreType.DMA((7,)),
            pltpu.SemaphoreType.DMA((4,)),
            pltpu.SemaphoreType.DMA((2, 4)),
            pltpu.SemaphoreType.DMA((2, 4)),
        ],
        compiler_params=pltpu.CompilerParams(
            collective_id=0, has_side_effects=True, vmem_limit_bytes=60 * 1024 * 1024,
        ),
        name="sections",
    )(state, source_in, counts, diffusivity, log_rate, activation, heat_release)
    return pl.pallas_call(
        second_kernel,
        out_shape=(whole,) * 2,
        in_specs=[outside] * 9,
        out_specs=(outside,) * 2,
        scratch_shapes=[
            field, field, field, field, field, *scalars,
            pltpu.SemaphoreType.DMA((9,)),
            pltpu.SemaphoreType.DMA((nx,)),
            pltpu.SemaphoreType.DMA((nx,)),
        ],
        compiler_params=pltpu.CompilerParams(vmem_limit_bytes=60 * 1024 * 1024),
        name="finish",
    )(state, first, early, late, partial, counts, log_rate, activation, heat_release)


def solution(mesh):
    grid = P(None, "gx", "gy", None)
    return jax.shard_map(
        local,
        mesh=mesh,
        in_specs=(grid, grid, P("gx", "gy"), P(), P(), P(), P()),
        out_specs=(grid, grid),
        check_vma=False,
    )
```

```python
import jax
import jax.numpy as jnp
import numpy as np
from jax import lax
from jax.experimental import pallas as pl
from jax.experimental.pallas import tpu as pltpu
from jax.sharding import PartitionSpec as P

time_step = 0.15
log2_e = 1.4426950408889634
early_steps = 2
reaction_table = (
    (3, 1, (4, 5)),
    (4, 0, (3, 5)),
    (5, 0, (3, 2)),
    (5, 5, (4, 2)),
    (3, 3, (0,)),
    (3, 5, (2,)),
    (4, 4, (1,)),
    (3, 4, (5,)),
    (3, 1, (6,)),
    (6, 3, (0, 1)),
    (6, 3, (5, 5)),
    (6, 4, (1, 5)),
    (6, 5, (2, 1)),
    (6, 6, (7, 1)),
    (7, 9, (5, 5)),
    (7, 3, (2, 5)),
    (7, 3, (6, 0)),
    (7, 4, (5, 6)),
    (7, 5, (6, 2)),
    (0, 9, (3, 3)),
    (2, 9, (3, 5)),
)
free_rows = (0, 1, 2, 4, 6, 7)
spanning = (7, 11, 14, 17, 19, 20)


def spanning_tables():
    change = np.zeros((9, 21))
    for reaction, (one, two, products) in enumerate(reaction_table):
        change[one, reaction] -= 1.0
        if two < 9:
            change[two, reaction] -= 1.0
        for product in products:
            change[product, reaction] += 1.0
    kept = change[list(free_rows)]
    inverse = np.round(np.linalg.inv(kept[:, list(spanning)]), 6)
    return inverse, np.round(inverse @ kept, 6)


def weighted(terms):
    total = None
    for weight, value in terms:
        if weight == 0:
            continue
        term = value if weight == 1 else value * float(weight)
        total = term if total is None else total + term
    return total


def heat_scalars(heat):
    inverse, spans = spanning_tables()
    base = [heat[r] for r in spanning]
    on_rows = [weighted([(inverse[i, j], base[i]) for i in range(6)]) for j in range(6)]
    on_reactions = {}
    for r in range(21):
        if r not in spanning:
            on_reactions[r] = weighted([(1.0, heat[r])] + [(-spans[i, r], base[i]) for i in range(6)])
    return on_rows, on_reactions


def prepare(temperature, stride, log_rate, activation):
    inverse_t = 1.0 / temperature
    return [jnp.exp2(log_rate[r] * log2_e - (activation[r] * log2_e) * inverse_t) * stride for r in range(21)]


def atoms(u):
    h2, o2, h2o, h, o, oh, ho2, h2o2 = u
    oxygen = 2.0 * (o2 + ho2 + h2o2) + h2o + o + oh
    surplus = 2.0 * (h2 - o2) + h2o + h - ho2 - o
    return oxygen, surplus


def substep(u, kept, k, active):
    h2, o2, h2o, h, o, oh, ho2, h2o2 = u
    oxygen, surplus = kept
    a, b, c, d, e, f, g = (h2, h2o, h, o, oh, ho2, h2o2)
    if active is not None:
        a, b, c, d, e, f, g = [jnp.where(active, v, 0.0) for v in (a, b, c, d, e, f, g)]
    p = {0: c * o2, 1: d * a, 2: e * a, 3: e * e, 4: c * c, 5: c * e, 6: d * d, 9: f * c, 12: f * e, 13: f * f,
         15: g * c, 18: g * e}
    w = {r: k[r] * v for r, v in p.items()}
    w[8] = k[8] * p[0]
    w[10] = k[10] * p[9]
    w[16] = k[16] * p[15]
    w[7] = k[7] * (c * d)
    w[11] = k[11] * (f * d)
    w[17] = k[17] * (g * d)
    w[14] = k[14] * g
    w[19] = k[19] * a
    w[20] = k[20] * b
    s1 = w[16] + w[17] + w[18]
    s2 = (w[9] + w[13]) + (w[11] + w[12])
    h2 = h2 + (((w[4] + w[9]) + (w[16] - w[1])) - (w[2] + w[19]))
    o2 = o2 + ((s2 + w[6]) - (w[0] + w[8]))
    h2o = h2o + (((w[2] + w[3]) + (w[5] + w[12])) + ((w[15] + w[18]) - w[20]))
    o = o + (((w[0] + w[3]) - (w[1] + w[7])) - ((w[6] + w[6]) + (w[11] + w[17])))
    ho2 = ho2 + (((s1 + w[8]) - s2) - (w[10] + w[13]))
    h2o2 = h2o2 + ((w[13] - s1) - (w[14] + w[15]))
    oh = ((oxygen - h2o) - o) - 2.0 * ((o2 + ho2) + h2o2)
    h = ((surplus - h2o) + (ho2 + o)) - 2.0 * (h2 - o2)
    return (h2, o2, h2o, h, o, oh, ho2, h2o2), p


def warmth(change, sums, k, heat):
    on_rows, on_reactions = heat_scalars(heat)
    rate = {r: on_reactions[r] * k[r] for r in on_reactions}
    rate[0] = rate[0] + rate.pop(8)
    rate[9] = rate[9] + rate.pop(10)
    rate[15] = rate[15] + rate.pop(16)
    terms = [rate[r] * total for r, total in sums.items()]
    terms += [weight * change[row] for weight, row in zip(on_rows, free_rows)]
    while len(terms) > 1:
        terms = [sum(terms[i + 1:i + 2], terms[i]) for i in range(0, len(terms), 2)]
    return terms[0]


def begin_chemistry(u, counts, stride, log_rate, activation, heat):
    k = prepare(u[9], stride, log_rate, activation)
    before = tuple(u[:8])
    kept = atoms(before)
    now, sums = substep(before, kept, k, None)
    for turn in range(1, early_steps):
        now, p = substep(now, kept, k, counts > float(turn))
        sums = {r: sums[r] + p[r] for r in sums}
    change = [after - start for after, start in zip(now, before)]
    return change + [jnp.zeros_like(u[9]), warmth(change, sums, k, heat)]


def finish_chemistry(parts, counts, stride, last, log_rate, activation, heat):
    number = len(parts)
    ks = [prepare(u[9], stride, log_rate, activation) for u, _ in parts]
    starts = [tuple(a + b for a, b in zip(u[:8], change[:8])) for u, change in parts]
    kept = [atoms(start) for start in starts]
    names = (0, 1, 2, 3, 4, 5, 6, 9, 12, 13, 15, 18)
    zero = jnp.zeros_like(counts)

    def turn(index, carry):
        active = counts > index.astype(jnp.float32)
        result = []
        for n in range(number):
            now, sums = carry[n]
            now, p = substep(now, kept[n], ks[n], active)
            result.append((now, tuple(total + p[r] for r, total in zip(names, sums))))
        return tuple(result)

    ends = lax.fori_loop(early_steps, last, turn, tuple((start, (zero,) * len(names)) for start in starts))
    results = []
    for n in range(number):
        now, sums = ends[n]
        more = [after - start for after, start in zip(now, starts[n])]
        warm = warmth(more, dict(zip(names, sums)), ks[n], heat)
        results.append(more + [zero, warm])
    return results


def block_numbers(counts, i, row_index, ny):
    number = jnp.zeros(row_index.shape, jnp.int32)
    for j in range(ny):
        number = jnp.where(row_index == j, counts[i, j], number)
    return number.astype(jnp.float32)


def first_kernel(
    state, source, counts_in, diffusivity_in, log_rate_in, activation_in, heat_in,
    first_out, early_out, late_out, next_out,
    st, src, first, early, late, nxt, counts, diffusivity, log_rate, activation, heat,
    fx1, fy1, fx2, fy2, hx1, hy1, hx2, hy2,
    load_sem, face_sem, store_sem, send_sem, recv_sem,
):
    rows, nx, ny, nz = st.shape
    x, size_x = lax.axis_index("gx"), lax.axis_size("gx")
    y, size_y = lax.axis_index("gy"), lax.axis_size("gy")
    neighbours = (
        {"gx": lax.rem(x + 1, size_x)},
        {"gx": lax.rem(x + size_x - 1, size_x)},
        {"gy": lax.rem(y + 1, size_y)},
        {"gy": lax.rem(y + size_y - 1, size_y)},
    )
    barrier = pltpu.get_barrier_semaphore()
    for device in neighbours:
        pl.semaphore_signal(barrier, inc=1, device_id=device, device_id_type=pl.DeviceIdType.MESH)
    pairs = (
        (state, st), (counts_in, counts), (log_rate_in, log_rate), (activation_in, activation), (heat_in, heat),
        (diffusivity_in, diffusivity), (source, src),
    )
    pieces = (
        (state.at[:, nx - 1], fx1.at[0]),
        (state.at[:, 0], fx1.at[1]),
        (state.at[:, :, ny - 1], fy1.at[0]),
        (state.at[:, :, 0], fy1.at[1]),
    )
    faces = [pltpu.make_async_copy(one, two, face_sem.at[n]) for n, (one, two) in enumerate(pieces)]
    loads = [pltpu.make_async_copy(one, two, load_sem.at[n]) for n, (one, two) in enumerate(pairs)]
    for load in faces + loads:
        load.start()
    for face in faces:
        face.wait()
    pl.semaphore_wait(barrier, 4)

    def exchange(face_x, face_y, halo_x, halo_y, turn):
        pieces = (
            (face_x.at[0], halo_x.at[0]),
            (face_x.at[1], halo_x.at[1]),
            (face_y.at[0], halo_y.at[0]),
            (face_y.at[1], halo_y.at[1]),
        )
        copies = []
        for place, (piece, device) in enumerate(zip(pieces, neighbours)):
            copies.append(pltpu.make_async_remote_copy(
                src_ref=piece[0], dst_ref=piece[1],
                send_sem=send_sem.at[turn, place], recv_sem=recv_sem.at[turn, place],
                device_id=device, device_id_type=pl.DeviceIdType.MESH,
            ))
        for place in (2, 3, 0, 1):
            copies[place].start()
        return copies

    first_copies = exchange(fx1, fy1, hx1, hy1, 0)
    row_index = lax.broadcasted_iota(jnp.int32, (ny, nz), 0)

    def laplace(field, halo_x, halo_y, k, i):
        here = field[k, i]
        before = halo_x[0, k] if i == 0 else field[k, i - 1]
        after = halo_x[1, k] if i == nx - 1 else field[k, i + 1]
        low = jnp.where(row_index == 0, halo_y[0, k, pl.ds(i, 1), :], pltpu.roll(here, 1, 0))
        high = jnp.where(row_index == ny - 1, halo_y[1, k, pl.ds(i, 1), :], pltpu.roll(here, ny - 1, 0))
        beside = (before + after) + (low + high) + (pltpu.roll(here, 1, 1) + pltpu.roll(here, nz - 1, 1))
        return beside - 6.0 * here

    def chemistry(field, into, scale=None):
        def group(i, carry):
            u = [field[s, i] for s in range(rows)]
            number = block_numbers(counts, i, row_index, ny)
            change = begin_chemistry(u, number, time_step / number, log_rate, activation, heat)
            for s in range(rows):
                into[s, i] = change[s] if scale is None else scale * change[s]
            return carry

        lax.fori_loop(0, nx, group, 0)

    for load in loads:
        load.wait()
    stores = [
        pltpu.make_async_copy(one, two, store_sem.at[n])
        for n, (one, two) in enumerate(((early, early_out), (first, first_out), (late, late_out), (nxt, next_out)))
    ]
    chemistry(st, early)
    stores[0].start()
    for copy in first_copies:
        copy.wait()

    def first_row(k, carry):
        spread = diffusivity[k]
        for i in range(nx):
            value = st[k, i] + time_step * (spread * laplace(st, hx1, hy1, k, i) + src[k, i])
            first[k, i] = value
            fy2[0, k, pl.ds(i, 1), :] = value[ny - 1:]
            fy2[1, k, pl.ds(i, 1), :] = value[:1]
            if i == nx - 1:
                fx2[0, k] = value
            if i == 0:
                fx2[1, k] = value
        return carry

    lax.fori_loop(0, rows, first_row, 0)
    second_copies = exchange(fx2, fy2, hx2, hy2, 1)
    stores[1].start()
    chemistry(first, late, 1.0 / time_step)
    stores[2].start()
    for copy in second_copies:
        copy.wait()

    def next_row(k, carry):
        weight = (0.5 * time_step) * diffusivity[k]
        for i in range(nx):
            held = 0.5 * ((st[k, i] + first[k, i]) + early[k, i])
            nxt[k, i] = held + weight * laplace(first, hx2, hy2, k, i)
        return carry

    lax.fori_loop(0, rows, next_row, 0)
    stores[3].start()
    for store in stores:
        store.wait()


def second_kernel(
    state, first_in, early_in, late_in, next_in, counts_in, log_rate_in, activation_in, heat_in,
    next_out, late_out,
    st, first, early, late, nxt, counts, log_rate, activation, heat,
    small_sem, load_sem, more_sem, next_sem, late_sem,
):
    rows, nx, ny, nz = st.shape
    pairs = ((counts_in, counts), (log_rate_in, log_rate), (activation_in, activation), (heat_in, heat))
    small = [pltpu.make_async_copy(one, two, small_sem.at[n]) for n, (one, two) in enumerate(pairs)]
    for load in small:
        load.start()

    def in_copies(i):
        return (
            pltpu.make_async_copy(next_in.at[:, i], nxt.at[:, i], load_sem.at[0, i]),
            pltpu.make_async_copy(late_in.at[:, i], late.at[:, i], load_sem.at[1, i]),
        )

    fields = ((state, st), (first_in, first), (early_in, early))
    more = [pltpu.make_async_copy(one, two, more_sem.at[n]) for n, (one, two) in enumerate(fields)]
    for i in range(nx):
        for copy in in_copies(i):
            copy.start()
    for load in small:
        load.wait()
    highest = counts[0, 0]
    for i in range(nx):
        for j in range(ny):
            highest = jnp.maximum(highest, counts[i, j])

    @pl.when(highest > early_steps)
    def _():
        for copy in more:
            copy.start()
        for copy in more:
            copy.wait()

    row_index = lax.broadcasted_iota(jnp.int32, (ny, nz), 0)

    def out_copies(i):
        return (
            pltpu.make_async_copy(nxt.at[:, i], next_out.at[:, i], next_sem.at[i]),
            pltpu.make_async_copy(late.at[:, i], late_out.at[:, i], late_sem.at[i]),
        )

    def group(i, carry):
        for copy in in_copies(i):
            copy.wait()
        last = counts[i, 0]
        for j in range(1, ny):
            last = jnp.maximum(last, counts[i, j])

        @pl.when(last > early_steps)
        def _():
            number = block_numbers(counts, i, row_index, ny)
            fields = ([st[s, i] for s in range(rows)], [first[s, i] for s in range(rows)])
            changes = ([early[s, i] for s in range(rows)], [late[s, i] * time_step for s in range(rows)])
            early_more, late_more = finish_chemistry(
                tuple(zip(fields, changes)), number, time_step / number, last, log_rate, activation, heat,
            )
            for s in range(rows):
                nxt[s, i] = nxt[s, i] + 0.5 * early_more[s]
                late[s, i] = late[s, i] + late_more[s] * (1.0 / time_step)

        for copy in out_copies(i):
            copy.start()
        return carry

    lax.fori_loop(0, nx, group, 0)
    for i in range(nx):
        for copy in out_copies(i):
            copy.wait()


def local(state, source_in, counts, diffusivity, log_rate, activation, heat_release):
    rows, nx, ny, nz = state.shape
    whole = jax.ShapeDtypeStruct(state.shape, jnp.float32)
    field = pltpu.VMEM(state.shape, jnp.float32)
    outside = pl.BlockSpec(memory_space=pl.ANY)
    scalars = [pltpu.SMEM(a.shape, a.dtype) for a in (counts, log_rate, activation, heat_release)]
    halo_x = pltpu.VMEM((2, rows, ny, nz), jnp.float32)
    halo_y = pltpu.VMEM((2, rows, nx, nz), jnp.float32)
    first, early, late, partial = pl.pallas_call(
        first_kernel,
        out_shape=(whole,) * 4,
        in_specs=[outside] * 7,
        out_specs=(outside,) * 4,
        scratch_shapes=[
            field, field, field, field, field, field,
            scalars[0], pltpu.SMEM(diffusivity.shape, jnp.float32), *scalars[1:],
            halo_x, halo_y, halo_x, halo_y, halo_x, halo_y, halo_x, halo_y,
            pltpu.SemaphoreType.DMA((7,)),
            pltpu.SemaphoreType.DMA((4,)),
            pltpu.SemaphoreType.DMA((4,)),
            pltpu.SemaphoreType.DMA((2, 4)),
            pltpu.SemaphoreType.DMA((2, 4)),
        ],
        compiler_params=pltpu.CompilerParams(
            collective_id=0, has_side_effects=True, vmem_limit_bytes=60 * 1024 * 1024,
        ),
        name="sections",
    )(state, source_in, counts, diffusivity, log_rate, activation, heat_release)
    return pl.pallas_call(
        second_kernel,
        out_shape=(whole,) * 2,
        in_specs=[outside] * 9,
        out_specs=(outside,) * 2,
        scratch_shapes=[
            field, field, field, field, field, *scalars,
            pltpu.SemaphoreType.DMA((4,)),
            pltpu.SemaphoreType.DMA((2, nx)),
            pltpu.SemaphoreType.DMA((3,)),
            pltpu.SemaphoreType.DMA((nx,)),
            pltpu.SemaphoreType.DMA((nx,)),
        ],
        compiler_params=pltpu.CompilerParams(vmem_limit_bytes=60 * 1024 * 1024),
        name="finish",
    )(state, first, early, late, partial, counts, log_rate, activation, heat_release)


def solution(mesh):
    grid = P(None, "gx", "gy", None)
    return jax.shard_map(
        local,
        mesh=mesh,
        in_specs=(grid, grid, P("gx", "gy"), P(), P(), P(), P()),
        out_specs=(grid, grid),
        check_vma=False,
    )
```

```python
import jax
import jax.numpy as jnp
import numpy as np
from jax import lax
from jax.experimental import pallas as pl
from jax.experimental.pallas import tpu as pltpu
from jax.sharding import PartitionSpec as P

time_step = 0.15
log2_e = 1.4426950408889634
most_steps = 8
late_steps = 2
together = 2
halves = 2
reaction_table = (
    (3, 1, (4, 5)),
    (4, 0, (3, 5)),
    (5, 0, (3, 2)),
    (5, 5, (4, 2)),
    (3, 3, (0,)),
    (3, 5, (2,)),
    (4, 4, (1,)),
    (3, 4, (5,)),
    (3, 1, (6,)),
    (6, 3, (0, 1)),
    (6, 3, (5, 5)),
    (6, 4, (1, 5)),
    (6, 5, (2, 1)),
    (6, 6, (7, 1)),
    (7, 9, (5, 5)),
    (7, 3, (2, 5)),
    (7, 3, (6, 0)),
    (7, 4, (5, 6)),
    (7, 5, (6, 2)),
    (0, 9, (3, 3)),
    (2, 9, (3, 5)),
)
free_rows = (0, 1, 2, 4, 6, 7)
spanning = (7, 11, 14, 17, 19, 20)


def spanning_tables():
    change = np.zeros((9, 21))
    for reaction, (one, two, products) in enumerate(reaction_table):
        change[one, reaction] -= 1.0
        if two < 9:
            change[two, reaction] -= 1.0
        for product in products:
            change[product, reaction] += 1.0
    kept = change[list(free_rows)]
    inverse = np.round(np.linalg.inv(kept[:, list(spanning)]), 6)
    return inverse, np.round(inverse @ kept, 6)


def weighted(terms):
    total = None
    for weight, value in terms:
        if weight == 0:
            continue
        term = value if weight == 1 else value * float(weight)
        total = term if total is None else total + term
    return total


def heat_scalars(heat):
    inverse, spans = spanning_tables()
    base = [heat[r] for r in spanning]
    on_rows = [weighted([(inverse[i, j], base[i]) for i in range(6)]) for j in range(6)]
    on_reactions = {}
    for r in range(21):
        if r not in spanning:
            on_reactions[r] = weighted([(1.0, heat[r])] + [(-spans[i, r], base[i]) for i in range(6)])
    return on_rows, on_reactions


def prepare(temperature, stride, log_rate, activation):
    inverse_t = 1.0 / temperature
    return [jnp.exp2(log_rate[r] * log2_e - (activation[r] * log2_e) * inverse_t) * stride for r in range(21)]


def atoms(u):
    h2, o2, h2o, h, o, oh, ho2, h2o2 = u
    oxygen = 2.0 * (o2 + ho2 + h2o2) + h2o + o + oh
    surplus = 2.0 * (h2 - o2) + h2o + h - ho2 - o
    return oxygen, surplus


def substep(u, kept, k, active):
    h2, o2, h2o, h, o, oh, ho2, h2o2 = u
    oxygen, surplus = kept
    a, b, c, d, e, f, g = (h2, h2o, h, o, oh, ho2, h2o2)
    if active is not None:
        a, b, c, d, e, f, g = [jnp.where(active, v, 0.0) for v in (a, b, c, d, e, f, g)]
    p = {0: c * o2, 1: d * a, 2: e * a, 3: e * e, 4: c * c, 5: c * e, 6: d * d, 9: f * c, 12: f * e, 13: f * f,
         15: g * c, 18: g * e}
    w = {r: k[r] * v for r, v in p.items()}
    w[8] = k[8] * p[0]
    w[10] = k[10] * p[9]
    w[16] = k[16] * p[15]
    w[7] = k[7] * (c * d)
    w[11] = k[11] * (f * d)
    w[17] = k[17] * (g * d)
    w[14] = k[14] * g
    w[19] = k[19] * a
    w[20] = k[20] * b
    s1 = w[16] + w[17] + w[18]
    s2 = (w[9] + w[13]) + (w[11] + w[12])
    h2 = h2 + (((w[4] + w[9]) + (w[16] - w[1])) - (w[2] + w[19]))
    o2 = o2 + ((s2 + w[6]) - (w[0] + w[8]))
    h2o = h2o + (((w[2] + w[3]) + (w[5] + w[12])) + ((w[15] + w[18]) - w[20]))
    o = o + (((w[0] + w[3]) - (w[1] + w[7])) - ((w[6] + w[6]) + (w[11] + w[17])))
    ho2 = ho2 + (((s1 + w[8]) - s2) - (w[10] + w[13]))
    h2o2 = h2o2 + ((w[13] - s1) - (w[14] + w[15]))
    oh = ((oxygen - h2o) - o) - 2.0 * ((o2 + ho2) + h2o2)
    h = ((surplus - h2o) + (ho2 + o)) - 2.0 * (h2 - o2)
    return (h2, o2, h2o, h, o, oh, ho2, h2o2), p


def warmth(change, sums, k, heat):
    on_rows, on_reactions = heat_scalars(heat)
    rate = {r: on_reactions[r] * k[r] for r in on_reactions}
    rate[0] = rate[0] + rate.pop(8)
    rate[9] = rate[9] + rate.pop(10)
    rate[15] = rate[15] + rate.pop(16)
    terms = [rate[r] * total for r, total in sums.items()]
    terms += [weight * change[row] for weight, row in zip(on_rows, free_rows)]
    while len(terms) > 1:
        terms = [sum(terms[i + 1:i + 2], terms[i]) for i in range(0, len(terms), 2)]
    return terms[0]


def chemistry(u, counts, stride, log_rate, activation, heat, done, upto):
    k = prepare(u[9], stride, log_rate, activation)
    before = tuple(u[:8])
    kept = atoms(before)
    now, sums = before, None
    for turn in range(done, upto):
        now, p = substep(now, kept, k, None if turn == 0 else counts > float(turn))
        sums = p if sums is None else {r: sums[r] + p[r] for r in sums}
    change = [after - start for after, start in zip(now, before)]
    return change + [jnp.zeros_like(u[9]), warmth(change, sums, k, heat)]


def block_numbers(counts, i, row_index, ny):
    number = jnp.zeros(row_index.shape, jnp.int32)
    for j in range(ny):
        number = jnp.where(row_index == j, counts[i, j], number)
    return number.astype(jnp.float32)


def first_kernel(
    state, source, counts_in, diffusivity_in, log_rate_in, activation_in, heat_in,
    first_out, late_out, next_out,
    st, src, first, held, late, nxt, counts, diffusivity, log_rate, activation, heat, numbers,
    fx, fy, hx1, hy1, hx2, hy2,
    load_sem, store_sem, send_sem, recv_sem,
):
    rows, nx, ny, nz = st.shape
    half = rows // halves
    x, size_x = lax.axis_index("gx"), lax.axis_size("gx")
    y, size_y = lax.axis_index("gy"), lax.axis_size("gy")
    neighbours = (
        {"gx": lax.rem(x + 1, size_x)},
        {"gx": lax.rem(x + size_x - 1, size_x)},
        {"gy": lax.rem(y + 1, size_y)},
        {"gy": lax.rem(y + size_y - 1, size_y)},
    )
    barrier = pltpu.get_barrier_semaphore()
    for device in neighbours:
        pl.semaphore_signal(barrier, inc=1, device_id=device, device_id_type=pl.DeviceIdType.MESH)
    pairs = (
        (state, st), (counts_in, counts), (log_rate_in, log_rate), (activation_in, activation), (heat_in, heat),
        (diffusivity_in, diffusivity), (source, src),
    )
    loads = [pltpu.make_async_copy(one, two, load_sem.at[n]) for n, (one, two) in enumerate(pairs)]
    for load in loads:
        load.start()
    pl.semaphore_wait(barrier, 4)

    def exchange(pieces, turn, part):
        copies = []
        for place, (piece, device) in enumerate(zip(pieces, neighbours)):
            copies.append(pltpu.make_async_remote_copy(
                src_ref=piece[0], dst_ref=piece[1],
                send_sem=send_sem.at[turn, part, place], recv_sem=recv_sem.at[turn, part, place],
                device_id=device, device_id_type=pl.DeviceIdType.MESH,
            ))
        for place in (2, 3, 0, 1):
            copies[place].start()
        return copies

    def span(part):
        return pl.ds(part * half, half)

    first_copies = [
        exchange((
            (state.at[span(part), nx - 1], hx1.at[0, span(part)]),
            (state.at[span(part), 0], hx1.at[1, span(part)]),
            (state.at[span(part), :, ny - 1], hy1.at[0, span(part)]),
            (state.at[span(part), :, 0], hy1.at[1, span(part)]),
        ), 0, part)
        for part in range(halves)
    ]
    row_index = lax.broadcasted_iota(jnp.int32, (ny, nz), 0)
    at_low, at_high = row_index == 0, row_index == ny - 1

    def inner_laplace(field, k, i):
        here = field[k, i]
        low = jnp.where(at_low, 0.0, pltpu.roll(here, 1, 0))
        high = jnp.where(at_high, 0.0, pltpu.roll(here, ny - 1, 0))
        beside = (low + high) + (pltpu.roll(here, 1, 1) + pltpu.roll(here, nz - 1, 1))
        if i > 0:
            beside = beside + field[k, i - 1]
        if i < nx - 1:
            beside = beside + field[k, i + 1]
        return beside - 6.0 * here

    def outer_laplace(halo_x, halo_y, k, i):
        low = jnp.where(at_low, halo_y[0, k, pl.ds(i, 1), :], 0.0)
        rest = jnp.where(at_high, halo_y[1, k, pl.ds(i, 1), :], low)
        if i == 0:
            rest = rest + halo_x[0, k]
        if i == nx - 1:
            rest = rest + halo_x[1, k]
        return rest

    def fields(field, i):
        part = pl.ds(i * together, together)
        u = [field[s, part] for s in range(rows)]
        return part, u, numbers[part]

    for load in loads:
        load.wait()
    for i in range(nx):
        numbers[i] = block_numbers(counts, i, row_index, ny)

    def early_group(i, carry):
        part, u, number = fields(st, i)
        change = chemistry(u, number, time_step / number, log_rate, activation, heat, 0, most_steps)
        for s in range(rows):
            held[s, part] = u[s] + 0.5 * change[s]
        return carry

    def first_inner(k, carry):
        weight = time_step * diffusivity[k]
        for i in range(nx):
            first[k, i] = (st[k, i] + time_step * src[k, i]) + weight * inner_laplace(st, k, i)
        return carry

    def first_outer(k, carry):
        weight = time_step * diffusivity[k]
        for i in range(nx):
            value = first[k, i] + weight * outer_laplace(hx1, hy1, k, i)
            first[k, i] = value
            fy[0, k, pl.ds(i, 1), :] = value[ny - 1:]
            fy[1, k, pl.ds(i, 1), :] = value[:1]
            if i == nx - 1:
                fx[0, k] = value
            if i == 0:
                fx[1, k] = value
        return carry

    lax.fori_loop(0, rows, first_inner, 0)
    lax.fori_loop(0, nx // together, early_group, 0)
    second_copies = []
    for part in range(halves):
        for copy in first_copies[part]:
            copy.wait()
        lax.fori_loop(part * half, part * half + half, first_outer, 0)
        second_copies.append(exchange((
            (fx.at[0, span(part)], hx2.at[0, span(part)]),
            (fx.at[1, span(part)], hx2.at[1, span(part)]),
            (fy.at[0, span(part)], hy2.at[0, span(part)]),
            (fy.at[1, span(part)], hy2.at[1, span(part)]),
        ), 1, part))
    first_store = pltpu.make_async_copy(first, first_out, store_sem.at[0])
    first_store.start()

    def late_group(i, carry):
        part, u, number = fields(first, i)
        change = chemistry(u, number, time_step / number, log_rate, activation, heat, 0, late_steps)
        for s in range(rows):
            late[s, part] = change[s] * (1.0 / time_step)
        return carry

    def next_inner(k, carry):
        weight = (0.5 * time_step) * diffusivity[k]
        for i in range(nx):
            nxt[k, i] = (held[k, i] + 0.5 * (first[k, i] - st[k, i])) + weight * inner_laplace(first, k, i)
        return carry

    def next_outer(k, carry):
        weight = (0.5 * time_step) * diffusivity[k]
        for i in range(nx):
            nxt[k, i] = nxt[k, i] + weight * outer_laplace(hx2, hy2, k, i)
        return carry

    lax.fori_loop(0, nx // together, late_group, 0)
    late_store = pltpu.make_async_copy(late, late_out, store_sem.at[1])
    late_store.start()
    lax.fori_loop(0, rows, next_inner, 0)
    stores = [first_store, late_store]
    for part in range(halves):
        for copy in second_copies[part]:
            copy.wait()
        lax.fori_loop(part * half, part * half + half, next_outer, 0)
        stores.append(pltpu.make_async_copy(nxt.at[span(part)], next_out.at[span(part)], store_sem.at[2 + part]))
        stores[-1].start()
    for store in stores:
        store.wait()


def second_kernel(
    first_in, late_in, next_in, counts_in, log_rate_in, activation_in, heat_in,
    next_out, late_out,
    first, late, counts, log_rate, activation, heat, small_sem, load_sem, copy_sem, late_sem,
):
    rows, nx, ny, nz = first.shape
    half = rows // halves
    pairs = ((counts_in, counts), (log_rate_in, log_rate), (activation_in, activation), (heat_in, heat))
    small = [pltpu.make_async_copy(one, two, small_sem.at[n]) for n, (one, two) in enumerate(pairs)]
    pairs = ((first_in, first), (late_in, late))
    loads = [pltpu.make_async_copy(one, two, load_sem.at[n]) for n, (one, two) in enumerate(pairs)]
    direct = []
    for n, (one, two) in enumerate(((next_in, next_out), (late_in, late_out))):
        for part in range(halves):
            span = pl.ds(part * half, half)
            direct.append(pltpu.make_async_copy(one.at[span], two.at[span], copy_sem.at[n, part]))
    for copy in small + direct + loads:
        copy.start()
    for copy in small:
        copy.wait()
    highest = counts[0, 0]
    for i in range(nx):
        for j in range(ny):
            highest = jnp.maximum(highest, counts[i, j])
    for copy in direct + loads:
        copy.wait()

    @pl.when(highest > late_steps)
    def _():
        row_index = lax.broadcasted_iota(jnp.int32, (ny, nz), 0)

        def out_copy(i):
            part = pl.ds(i * together, together)
            return pltpu.make_async_copy(late.at[:, part], late_out.at[:, part], late_sem.at[i])

        def group(i, carry):
            part = pl.ds(i * together, together)
            number = jnp.stack([block_numbers(counts, i * together + n, row_index, ny) for n in range(together)])
            u = [first[s, part] for s in range(rows)]
            ready = [late[s, part] for s in range(rows)]
            now = [u[s] + time_step * ready[s] for s in range(8)] + u[8:]
            more = chemistry(now, number, time_step / number, log_rate, activation, heat, late_steps, most_steps)
            for s in range(rows):
                late[s, part] = ready[s] + more[s] * (1.0 / time_step)
            out_copy(i).start()
            return carry

        lax.fori_loop(0, nx // together, group, 0)
        for i in range(nx // together):
            out_copy(i).wait()


def local(state, source_in, counts, diffusivity, log_rate, activation, heat_release):
    rows, nx, ny, nz = state.shape
    whole = jax.ShapeDtypeStruct(state.shape, jnp.float32)
    field = pltpu.VMEM(state.shape, jnp.float32)
    outside = pl.BlockSpec(memory_space=pl.ANY)
    scalars = [pltpu.SMEM(a.shape, a.dtype) for a in (counts, log_rate, activation, heat_release)]
    halo_x = pltpu.VMEM((2, rows, ny, nz), jnp.float32)
    halo_y = pltpu.VMEM((2, rows, nx, nz), jnp.float32)
    first, late, partial = pl.pallas_call(
        first_kernel,
        out_shape=(whole,) * 3,
        in_specs=[outside] * 7,
        out_specs=(outside,) * 3,
        scratch_shapes=[
            field, field, field, field, field, field,
            scalars[0], pltpu.SMEM(diffusivity.shape, jnp.float32), *scalars[1:],
            pltpu.VMEM((nx, ny, nz), jnp.float32),
            halo_x, halo_y, halo_x, halo_y, halo_x, halo_y,
            pltpu.SemaphoreType.DMA((7,)),
            pltpu.SemaphoreType.DMA((2 + halves,)),
            pltpu.SemaphoreType.DMA((2, halves, 4)),
            pltpu.SemaphoreType.DMA((2, halves, 4)),
        ],
        compiler_params=pltpu.CompilerParams(
            collective_id=0, has_side_effects=True, vmem_limit_bytes=60 * 1024 * 1024,
        ),
        name="sections",
    )(state, source_in, counts, diffusivity, log_rate, activation, heat_release)
    return pl.pallas_call(
        second_kernel,
        out_shape=(whole,) * 2,
        in_specs=[outside] * 7,
        out_specs=(outside,) * 2,
        scratch_shapes=[
            field, field, *scalars,
            pltpu.SemaphoreType.DMA((4,)),
            pltpu.SemaphoreType.DMA((2,)),
            pltpu.SemaphoreType.DMA((2, halves)),
            pltpu.SemaphoreType.DMA((nx // together,)),
        ],
        compiler_params=pltpu.CompilerParams(vmem_limit_bytes=60 * 1024 * 1024),
        name="finish",
    )(first, late, partial, counts, log_rate, activation, heat_release)


def solution(mesh):
    grid = P(None, "gx", "gy", None)
    return jax.shard_map(
        local,
        mesh=mesh,
        in_specs=(grid, grid, P("gx", "gy"), P(), P(), P(), P()),
        out_specs=(grid, grid),
        check_vma=False,
    )
```

```python
import jax
import jax.numpy as jnp
import numpy as np
from jax import lax
from jax.experimental import pallas as pl
from jax.experimental.pallas import tpu as pltpu
from jax.sharding import PartitionSpec as P

time_step = 0.15
log2_e = 1.4426950408889634
most_steps = 8
late_steps = 2
together = 2
reaction_table = (
    (3, 1, (4, 5)),
    (4, 0, (3, 5)),
    (5, 0, (3, 2)),
    (5, 5, (4, 2)),
    (3, 3, (0,)),
    (3, 5, (2,)),
    (4, 4, (1,)),
    (3, 4, (5,)),
    (3, 1, (6,)),
    (6, 3, (0, 1)),
    (6, 3, (5, 5)),
    (6, 4, (1, 5)),
    (6, 5, (2, 1)),
    (6, 6, (7, 1)),
    (7, 9, (5, 5)),
    (7, 3, (2, 5)),
    (7, 3, (6, 0)),
    (7, 4, (5, 6)),
    (7, 5, (6, 2)),
    (0, 9, (3, 3)),
    (2, 9, (3, 5)),
)
free_rows = (0, 1, 2, 4, 6, 7)
spanning = (7, 11, 14, 17, 19, 20)


def spanning_tables():
    change = np.zeros((9, 21))
    for reaction, (one, two, products) in enumerate(reaction_table):
        change[one, reaction] -= 1.0
        if two < 9:
            change[two, reaction] -= 1.0
        for product in products:
            change[product, reaction] += 1.0
    kept = change[list(free_rows)]
    inverse = np.round(np.linalg.inv(kept[:, list(spanning)]), 6)
    return inverse, np.round(inverse @ kept, 6)


def weighted(terms):
    total = None
    for weight, value in terms:
        if weight == 0:
            continue
        term = value if weight == 1 else value * float(weight)
        total = term if total is None else total + term
    return total


def heat_scalars(heat):
    inverse, spans = spanning_tables()
    base = [heat[r] for r in spanning]
    on_rows = [weighted([(inverse[i, j], base[i]) for i in range(6)]) for j in range(6)]
    on_reactions = {}
    for r in range(21):
        if r not in spanning:
            on_reactions[r] = weighted([(1.0, heat[r])] + [(-spans[i, r], base[i]) for i in range(6)])
    return on_rows, on_reactions


def prepare(temperature, stride, log_rate, activation):
    inverse_t = 1.0 / temperature
    return [jnp.exp2(log_rate[r] * log2_e - (activation[r] * log2_e) * inverse_t) * stride for r in range(21)]


def atoms(u):
    h2, o2, h2o, h, o, oh, ho2, h2o2 = u
    oxygen = 2.0 * (o2 + ho2 + h2o2) + h2o + o + oh
    surplus = 2.0 * (h2 - o2) + h2o + h - ho2 - o
    return oxygen, surplus


def substep(u, kept, k, active):
    h2, o2, h2o, h, o, oh, ho2, h2o2 = u
    oxygen, surplus = kept
    a, b, c, d, e, f, g = (h2, h2o, h, o, oh, ho2, h2o2)
    if active is not None:
        a, b, c, d, e, f, g = [jnp.where(active, v, 0.0) for v in (a, b, c, d, e, f, g)]
    p = {0: c * o2, 1: d * a, 2: e * a, 3: e * e, 4: c * c, 5: c * e, 6: d * d, 9: f * c, 12: f * e, 13: f * f,
         15: g * c, 18: g * e}
    w = {r: k[r] * v for r, v in p.items()}
    w[8] = k[8] * p[0]
    w[10] = k[10] * p[9]
    w[16] = k[16] * p[15]
    w[7] = k[7] * (c * d)
    w[11] = k[11] * (f * d)
    w[17] = k[17] * (g * d)
    w[14] = k[14] * g
    w[19] = k[19] * a
    w[20] = k[20] * b
    s1 = w[16] + w[17] + w[18]
    s2 = (w[9] + w[13]) + (w[11] + w[12])
    h2 = h2 + (((w[4] + w[9]) + (w[16] - w[1])) - (w[2] + w[19]))
    o2 = o2 + ((s2 + w[6]) - (w[0] + w[8]))
    h2o = h2o + (((w[2] + w[3]) + (w[5] + w[12])) + ((w[15] + w[18]) - w[20]))
    o = o + (((w[0] + w[3]) - (w[1] + w[7])) - ((w[6] + w[6]) + (w[11] + w[17])))
    ho2 = ho2 + (((s1 + w[8]) - s2) - (w[10] + w[13]))
    h2o2 = h2o2 + ((w[13] - s1) - (w[14] + w[15]))
    oh = ((oxygen - h2o) - o) - 2.0 * ((o2 + ho2) + h2o2)
    h = ((surplus - h2o) + (ho2 + o)) - 2.0 * (h2 - o2)
    return (h2, o2, h2o, h, o, oh, ho2, h2o2), p


def warmth(change, sums, k, heat):
    on_rows, on_reactions = heat_scalars(heat)
    rate = {r: on_reactions[r] * k[r] for r in on_reactions}
    rate[0] = rate[0] + rate.pop(8)
    rate[9] = rate[9] + rate.pop(10)
    rate[15] = rate[15] + rate.pop(16)
    terms = [rate[r] * total for r, total in sums.items()]
    terms += [weight * change[row] for weight, row in zip(on_rows, free_rows)]
    while len(terms) > 1:
        terms = [sum(terms[i + 1:i + 2], terms[i]) for i in range(0, len(terms), 2)]
    return terms[0]


def chemistry(u, counts, stride, log_rate, activation, heat, done, upto):
    k = prepare(u[9], stride, log_rate, activation)
    before = tuple(u[:8])
    kept = atoms(before)
    now, sums = before, None
    for turn in range(done, upto):
        now, p = substep(now, kept, k, None if turn == 0 else counts > float(turn))
        sums = p if sums is None else {r: sums[r] + p[r] for r in sums}
    change = [after - start for after, start in zip(now, before)]
    return change + [jnp.zeros_like(u[9]), warmth(change, sums, k, heat)]


def block_numbers(counts, i, row_index, ny):
    number = jnp.zeros(row_index.shape, jnp.int32)
    for j in range(ny):
        number = jnp.where(row_index == j, counts[i, j], number)
    return number.astype(jnp.float32)


def first_kernel(
    state, source, counts_in, diffusivity_in, log_rate_in, activation_in, heat_in,
    first_out, next_out,
    st, src, first, nxt, counts, diffusivity, log_rate, activation, heat, numbers,
    own_y, fx, fy, hx1, hy1, corners, hx2, hy2,
    load_sem, store_sem, send_sem, recv_sem,
):
    rows, nx, ny, nz = st.shape
    x, size_x = lax.axis_index("gx"), lax.axis_size("gx")
    y, size_y = lax.axis_index("gy"), lax.axis_size("gy")
    x_up, x_down = lax.rem(x + 1, size_x), lax.rem(x + size_x - 1, size_x)
    y_up, y_down = lax.rem(y + 1, size_y), lax.rem(y + size_y - 1, size_y)
    sides = ((x_up, y), (x_down, y), (x, y_up), (x, y_down))
    diagonals = ((x_up, y_up), (x_up, y_down), (x_down, y_up), (x_down, y_down))
    barrier = pltpu.get_barrier_semaphore()
    for device in diagonals + sides:
        pl.semaphore_signal(barrier, inc=1, device_id=device, device_id_type=pl.DeviceIdType.MESH)
    pairs = (
        (state, st), (source, src), (diffusivity_in, diffusivity),
        (counts_in, counts), (log_rate_in, log_rate), (activation_in, activation), (heat_in, heat),
        (state.at[:, :, 0], own_y.at[0]), (state.at[:, :, ny - 1], own_y.at[1]),
    )
    loads = [pltpu.make_async_copy(one, two, load_sem.at[n]) for n, (one, two) in enumerate(pairs)]
    for load in loads:
        load.start()

    def send(pieces, devices, base):
        copies = []
        for place, (piece, device) in enumerate(zip(pieces, devices)):
            copies.append(pltpu.make_async_remote_copy(
                src_ref=piece[0], dst_ref=piece[1],
                send_sem=send_sem.at[base + place], recv_sem=recv_sem.at[base + place],
                device_id=device, device_id_type=pl.DeviceIdType.MESH,
            ))
        for copy in copies[::-1]:
            copy.start()
        return copies

    pl.semaphore_wait(barrier, 8)
    state_copies = send((
        (state.at[:, nx - 1], hx1.at[0]),
        (state.at[:, 0], hx1.at[1]),
        (state.at[:, :, ny - 1], hy1.at[0]),
        (state.at[:, :, 0], hy1.at[1]),
    ), sides, 0)
    corner_copies = send((
        (state.at[:, nx - 1, ny - 1], corners.at[0]),
        (state.at[:, nx - 1, 0], corners.at[1]),
        (state.at[:, 0, ny - 1], corners.at[2]),
        (state.at[:, 0, 0], corners.at[3]),
    ), diagonals, 4)

    row_index = lax.broadcasted_iota(jnp.int32, (ny, nz), 0)
    at_low, at_high = row_index == 0, row_index == ny - 1

    def inner_laplace(field, k, i):
        here = field[k, i]
        low = jnp.where(at_low, 0.0, pltpu.roll(here, 1, 0))
        high = jnp.where(at_high, 0.0, pltpu.roll(here, ny - 1, 0))
        beside = (low + high) + (pltpu.roll(here, 1, 1) + pltpu.roll(here, nz - 1, 1))
        if i > 0:
            beside = beside + field[k, i - 1]
        if i < nx - 1:
            beside = beside + field[k, i + 1]
        return beside - 6.0 * here

    def outer_laplace(halo_x, halo_y, k, i):
        low = jnp.where(at_low, halo_y[0, k, pl.ds(i, 1), :], 0.0)
        rest = jnp.where(at_high, halo_y[1, k, pl.ds(i, 1), :], low)
        if i == 0:
            rest = rest + halo_x[0, k]
        if i == nx - 1:
            rest = rest + halo_x[1, k]
        return rest

    def first_inner(k, carry):
        weight = time_step * diffusivity[k]
        for i in range(nx):
            value = (st[k, i] + time_step * src[k, i]) + weight * inner_laplace(st, k, i)
            first[k, i] = value
            fy[0, k, pl.ds(i, 1), :] = value[ny - 1:]
            fy[1, k, pl.ds(i, 1), :] = value[:1]
            if i == nx - 1:
                fx[0, k] = value
            if i == 0:
                fx[1, k] = value
        return carry

    for load in loads[:3]:
        load.wait()
    lax.fori_loop(0, rows, first_inner, 0)
    first_copies = send((
        (fx.at[0], hx2.at[0]), (fx.at[1], hx2.at[1]), (fy.at[0], hy2.at[0]), (fy.at[1], hy2.at[1]),
    ), sides, 8)

    for load in loads[3:]:
        load.wait()
    for i in range(nx):
        numbers[i] = block_numbers(counts, i, row_index, ny)

    def early_group(i, carry):
        part = pl.ds(i * together, together)
        u = [st[s, part] for s in range(rows)]
        number = numbers[part]
        change = chemistry(u, number, time_step / number, log_rate, activation, heat, 0, most_steps)
        for s in range(rows):
            nxt[s, part] = 0.5 * (u[s] + change[s])
        return carry

    lax.fori_loop(0, nx // together, early_group, 0)

    def first_outer(k, carry):
        weight = time_step * diffusivity[k]
        for i in range(nx):
            first[k, i] = first[k, i] + weight * outer_laplace(hx1, hy1, k, i)
        return carry

    for copy in state_copies:
        copy.wait()
    lax.fori_loop(0, rows, first_outer, 0)
    first_store = pltpu.make_async_copy(first, first_out, store_sem.at[0])
    first_store.start()

    def next_inner(k, carry):
        weight = (0.5 * time_step) * diffusivity[k]
        for i in range(nx):
            nxt[k, i] = (nxt[k, i] + 0.5 * first[k, i]) + weight * inner_laplace(first, k, i)
        return carry

    lax.fori_loop(0, rows, next_inner, 0)
    for copy in corner_copies + first_copies:
        copy.wait()

    side_index = lax.broadcasted_iota(jnp.int32, (nx, nz), 0)

    def next_outer(k, carry):
        weight = time_step * diffusivity[k]
        corner = [corners[n, pl.ds(k, 1), :] for n in range(4)]
        for n, plane in ((0, st[k, 0]), (1, st[k, nx - 1])):
            low = jnp.where(at_low, corner[2 * n], 0.0)
            rest = jnp.where(at_high, corner[2 * n + 1], low)
            hx2[n, k] = hx2[n, k] + weight * (plane + rest)
        for n in range(2):
            low = jnp.where(side_index == 0, corner[n], 0.0)
            rest = jnp.where(side_index == nx - 1, corner[2 + n], low)
            hy2[n, k] = hy2[n, k] + weight * (own_y[n, k] + rest)
        for i in range(nx):
            nxt[k, i] = nxt[k, i] + (0.5 * weight) * outer_laplace(hx2, hy2, k, i)
        return carry

    lax.fori_loop(0, rows, next_outer, 0)
    next_store = pltpu.make_async_copy(nxt, next_out, store_sem.at[1])
    next_store.start()
    first_store.wait()
    next_store.wait()


def second_kernel(
    first_in, next_in, counts_in, log_rate_in, activation_in, heat_in,
    next_out, late_out,
    first, nxt, late, counts, log_rate, activation, heat, small_sem, load_sem, next_sem, late_sem,
):
    rows, nx, ny, nz = first.shape
    groups = nx // together
    pairs = ((counts_in, counts), (log_rate_in, log_rate), (activation_in, activation), (heat_in, heat))
    small = [pltpu.make_async_copy(one, two, small_sem.at[n]) for n, (one, two) in enumerate(pairs)]

    def span(i):
        return pl.ds(i * together, together)

    def first_load(i):
        return pltpu.make_async_copy(first_in.at[:, span(i)], first.at[:, span(i)], load_sem.at[i])

    def late_store(i):
        return pltpu.make_async_copy(late.at[:, span(i)], late_out.at[:, span(i)], late_sem.at[i])

    next_load = pltpu.make_async_copy(next_in, nxt, next_sem.at[0])
    next_store = pltpu.make_async_copy(nxt, next_out, next_sem.at[1])
    for copy in small:
        copy.start()
    for i in range(groups):
        first_load(i).start()
    next_load.start()
    for copy in small:
        copy.wait()
    row_index = lax.broadcasted_iota(jnp.int32, (ny, nz), 0)

    def group(i, carry):
        last = counts[i * together, 0]
        for n in range(together):
            for j in range(ny):
                last = jnp.maximum(last, counts[i * together + n, j])
        number = jnp.stack([block_numbers(counts, i * together + n, row_index, ny) for n in range(together)])
        first_load(i).wait()

        def run(upto):
            u = [first[s, span(i)] for s in range(rows)]
            change = chemistry(u, number, time_step / number, log_rate, activation, heat, 0, upto)
            for s in range(rows):
                late[s, span(i)] = change[s] * (1.0 / time_step)

        @pl.when(last <= late_steps)
        def _():
            run(late_steps)

        @pl.when(last > late_steps)
        def _():
            run(most_steps)

        late_store(i).start()

        @pl.when(i == 0)
        def _():
            next_load.wait()
            next_store.start()

        return carry

    lax.fori_loop(0, groups, group, 0)
    next_store.wait()
    for i in range(groups):
        late_store(i).wait()


def local(state, source_in, counts, diffusivity, log_rate, activation, heat_release):
    rows, nx, ny, nz = state.shape
    whole = jax.ShapeDtypeStruct(state.shape, jnp.float32)
    field = pltpu.VMEM(state.shape, jnp.float32)
    outside = pl.BlockSpec(memory_space=pl.ANY)
    scalars = [pltpu.SMEM(a.shape, a.dtype) for a in (counts, log_rate, activation, heat_release)]
    halo_x = pltpu.VMEM((2, rows, ny, nz), jnp.float32)
    halo_y = pltpu.VMEM((2, rows, nx, nz), jnp.float32)
    first, partial = pl.pallas_call(
        first_kernel,
        out_shape=(whole,) * 2,
        in_specs=[outside] * 7,
        out_specs=(outside,) * 2,
        scratch_shapes=[
            field, field, field, field,
            scalars[0], pltpu.SMEM(diffusivity.shape, jnp.float32), *scalars[1:],
            pltpu.VMEM((nx, ny, nz), jnp.float32),
            halo_y, halo_x, halo_y, halo_x, halo_y, pltpu.VMEM((4, rows, nz), jnp.float32), halo_x, halo_y,
            pltpu.SemaphoreType.DMA((9,)),
            pltpu.SemaphoreType.DMA((2,)),
            pltpu.SemaphoreType.DMA((12,)),
            pltpu.SemaphoreType.DMA((12,)),
        ],
        compiler_params=pltpu.CompilerParams(
            collective_id=0, has_side_effects=True, vmem_limit_bytes=60 * 1024 * 1024,
        ),
        name="sections",
    )(state, source_in, counts, diffusivity, log_rate, activation, heat_release)
    return pl.pallas_call(
        second_kernel,
        out_shape=(whole,) * 2,
        in_specs=[outside] * 6,
        out_specs=(outside,) * 2,
        scratch_shapes=[
            field, field, field, *scalars,
            pltpu.SemaphoreType.DMA((4,)),
            pltpu.SemaphoreType.DMA((nx // together,)),
            pltpu.SemaphoreType.DMA((2,)),
            pltpu.SemaphoreType.DMA((nx // together,)),
        ],
        compiler_params=pltpu.CompilerParams(vmem_limit_bytes=60 * 1024 * 1024),
        name="finish",
    )(first, partial, counts, log_rate, activation, heat_release)


def solution(mesh):
    grid = P(None, "gx", "gy", None)
    return jax.shard_map(
        local,
        mesh=mesh,
        in_specs=(grid, grid, P("gx", "gy"), P(), P(), P(), P()),
        out_specs=(grid, grid),
        check_vma=False,
    )
```

```python
import jax
import jax.numpy as jnp
import numpy as np
from jax import lax
from jax.experimental import pallas as pl
from jax.experimental.pallas import tpu as pltpu
from jax.sharding import PartitionSpec as P

time_step = 0.15
log2_e = 1.4426950408889634
most_steps = 8
late_steps = 2
together = 2
reaction_table = (
    (3, 1, (4, 5)),
    (4, 0, (3, 5)),
    (5, 0, (3, 2)),
    (5, 5, (4, 2)),
    (3, 3, (0,)),
    (3, 5, (2,)),
    (4, 4, (1,)),
    (3, 4, (5,)),
    (3, 1, (6,)),
    (6, 3, (0, 1)),
    (6, 3, (5, 5)),
    (6, 4, (1, 5)),
    (6, 5, (2, 1)),
    (6, 6, (7, 1)),
    (7, 9, (5, 5)),
    (7, 3, (2, 5)),
    (7, 3, (6, 0)),
    (7, 4, (5, 6)),
    (7, 5, (6, 2)),
    (0, 9, (3, 3)),
    (2, 9, (3, 5)),
)
free_rows = (0, 1, 2, 4, 6, 7)
spanning = (7, 11, 14, 17, 19, 20)


def spanning_tables():
    change = np.zeros((9, 21))
    for reaction, (one, two, products) in enumerate(reaction_table):
        change[one, reaction] -= 1.0
        if two < 9:
            change[two, reaction] -= 1.0
        for product in products:
            change[product, reaction] += 1.0
    kept = change[list(free_rows)]
    inverse = np.round(np.linalg.inv(kept[:, list(spanning)]), 6)
    return inverse, np.round(inverse @ kept, 6)


def weighted(terms):
    total = None
    for weight, value in terms:
        if weight == 0:
            continue
        term = value if weight == 1 else value * float(weight)
        total = term if total is None else total + term
    return total


def heat_scalars(heat):
    inverse, spans = spanning_tables()
    base = [heat[r] for r in spanning]
    on_rows = [weighted([(inverse[i, j], base[i]) for i in range(6)]) for j in range(6)]
    on_reactions = {}
    for r in range(21):
        if r not in spanning:
            on_reactions[r] = weighted([(1.0, heat[r])] + [(-spans[i, r], base[i]) for i in range(6)])
    return on_rows, on_reactions


def prepare(temperature, stride, log_rate, activation):
    inverse_t = 1.0 / temperature
    return [jnp.exp2(log_rate[r] * log2_e - (activation[r] * log2_e) * inverse_t) * stride for r in range(21)]


def atoms(u):
    h2, o2, h2o, h, o, oh, ho2, h2o2 = u
    oxygen = 2.0 * (o2 + ho2 + h2o2) + h2o + o + oh
    surplus = 2.0 * (h2 - o2) + h2o + h - ho2 - o
    return oxygen, surplus


def substep(u, kept, k, active):
    h2, o2, h2o, h, o, oh, ho2, h2o2 = u
    oxygen, surplus = kept
    a, b, c, d, e, f, g = (h2, h2o, h, o, oh, ho2, h2o2)
    if active is not None:
        a, b, c, d, e, f, g = [jnp.where(active, v, 0.0) for v in (a, b, c, d, e, f, g)]
    p = {0: c * o2, 1: d * a, 2: e * a, 3: e * e, 4: c * c, 5: c * e, 6: d * d, 9: f * c, 12: f * e, 13: f * f,
         15: g * c, 18: g * e}
    w = {r: k[r] * v for r, v in p.items()}
    w[8] = k[8] * p[0]
    w[10] = k[10] * p[9]
    w[16] = k[16] * p[15]
    w[7] = k[7] * (c * d)
    w[11] = k[11] * (f * d)
    w[17] = k[17] * (g * d)
    w[14] = k[14] * g
    w[19] = k[19] * a
    w[20] = k[20] * b
    s1 = w[16] + w[17] + w[18]
    s2 = (w[9] + w[13]) + (w[11] + w[12])
    h2 = h2 + (((w[4] + w[9]) + (w[16] - w[1])) - (w[2] + w[19]))
    o2 = o2 + ((s2 + w[6]) - (w[0] + w[8]))
    h2o = h2o + (((w[2] + w[3]) + (w[5] + w[12])) + ((w[15] + w[18]) - w[20]))
    o = o + (((w[0] + w[3]) - (w[1] + w[7])) - ((w[6] + w[6]) + (w[11] + w[17])))
    ho2 = ho2 + (((s1 + w[8]) - s2) - (w[10] + w[13]))
    h2o2 = h2o2 + ((w[13] - s1) - (w[14] + w[15]))
    oh = ((oxygen - h2o) - o) - 2.0 * ((o2 + ho2) + h2o2)
    h = ((surplus - h2o) + (ho2 + o)) - 2.0 * (h2 - o2)
    return (h2, o2, h2o, h, o, oh, ho2, h2o2), p


def warmth(change, sums, k, heat):
    on_rows, on_reactions = heat_scalars(heat)
    rate = {r: on_reactions[r] * k[r] for r in on_reactions}
    rate[0] = rate[0] + rate.pop(8)
    rate[9] = rate[9] + rate.pop(10)
    rate[15] = rate[15] + rate.pop(16)
    terms = [rate[r] * total for r, total in sums.items()]
    terms += [weight * change[row] for weight, row in zip(on_rows, free_rows)]
    while len(terms) > 1:
        terms = [sum(terms[i + 1:i + 2], terms[i]) for i in range(0, len(terms), 2)]
    return terms[0]


def chemistry(u, counts, stride, log_rate, activation, heat, done, upto):
    k = prepare(u[9], stride, log_rate, activation)
    before = tuple(u[:8])
    kept = atoms(before)
    now, sums = before, None
    for turn in range(done, upto):
        now, p = substep(now, kept, k, None if turn == 0 else counts > float(turn))
        sums = p if sums is None else {r: sums[r] + p[r] for r in sums}
    change = [after - start for after, start in zip(now, before)]
    return change + [jnp.zeros_like(u[9]), warmth(change, sums, k, heat)]


def block_numbers(counts, i, row_index, ny):
    number = jnp.zeros(row_index.shape, jnp.int32)
    for j in range(ny):
        number = jnp.where(row_index == j, counts[i, j], number)
    return number.astype(jnp.float32)


def outer_laplace(halo_x, halo_y, k, i, at_low, at_high):
    last = halo_y.shape[2] - 1
    low = jnp.where(at_low, halo_y[0, k, pl.ds(i, 1), :], 0.0)
    rest = jnp.where(at_high, halo_y[1, k, pl.ds(i, 1), :], low)
    if i == 0:
        rest = rest + halo_x[0, k]
    if i == last:
        rest = rest + halo_x[1, k]
    return rest


def first_kernel(
    state, source, counts_in, diffusivity_in, log_rate_in, activation_in, heat_in,
    first_out, next_out, hx2, hy2,
    st, src, first, nxt, counts, diffusivity, log_rate, activation, heat, numbers,
    fx, fy, hx1, hy1, corners,
    load_sem, store_sem, send_sem, recv_sem,
):
    rows, nx, ny, nz = st.shape
    x, size_x = lax.axis_index("gx"), lax.axis_size("gx")
    y, size_y = lax.axis_index("gy"), lax.axis_size("gy")
    x_up, x_down = lax.rem(x + 1, size_x), lax.rem(x + size_x - 1, size_x)
    y_up, y_down = lax.rem(y + 1, size_y), lax.rem(y + size_y - 1, size_y)
    sides = ((x_up, y), (x_down, y), (x, y_up), (x, y_down))
    diagonals = ((x_up, y_up), (x_up, y_down), (x_down, y_up), (x_down, y_down))
    barrier = pltpu.get_barrier_semaphore()
    for device in diagonals + sides:
        pl.semaphore_signal(barrier, inc=1, device_id=device, device_id_type=pl.DeviceIdType.MESH)
    pairs = (
        (state, st), (source, src), (diffusivity_in, diffusivity),
        (counts_in, counts), (log_rate_in, log_rate), (activation_in, activation), (heat_in, heat),
    )
    loads = [pltpu.make_async_copy(one, two, load_sem.at[n]) for n, (one, two) in enumerate(pairs)]
    for load in loads:
        load.start()

    def send(pieces, devices, base):
        copies = []
        for place, (piece, device) in enumerate(zip(pieces, devices)):
            copies.append(pltpu.make_async_remote_copy(
                src_ref=piece[0], dst_ref=piece[1],
                send_sem=send_sem.at[base + place], recv_sem=recv_sem.at[base + place],
                device_id=device, device_id_type=pl.DeviceIdType.MESH,
            ))
        for copy in copies[::-1]:
            copy.start()
        return copies

    pl.semaphore_wait(barrier, 8)
    state_copies = send((
        (state.at[:, nx - 1], hx1.at[0]),
        (state.at[:, 0], hx1.at[1]),
        (state.at[:, :, ny - 1], hy1.at[0]),
        (state.at[:, :, 0], hy1.at[1]),
    ), sides, 0)
    corner_copies = send((
        (state.at[:, nx - 1, ny - 1], corners.at[0]),
        (state.at[:, nx - 1, 0], corners.at[1]),
        (state.at[:, 0, ny - 1], corners.at[2]),
        (state.at[:, 0, 0], corners.at[3]),
    ), diagonals, 4)

    row_index = lax.broadcasted_iota(jnp.int32, (ny, nz), 0)
    at_low, at_high = row_index == 0, row_index == ny - 1

    def inner_laplace(field, k, i):
        here = field[k, i]
        low = jnp.where(at_low, 0.0, pltpu.roll(here, 1, 0))
        high = jnp.where(at_high, 0.0, pltpu.roll(here, ny - 1, 0))
        beside = (low + high) + (pltpu.roll(here, 1, 1) + pltpu.roll(here, nz - 1, 1))
        if i > 0:
            beside = beside + field[k, i - 1]
        if i < nx - 1:
            beside = beside + field[k, i + 1]
        return beside - 6.0 * here

    def first_inner(k, carry):
        weight = time_step * diffusivity[k]
        for i in range(nx):
            value = (st[k, i] + time_step * src[k, i]) + weight * inner_laplace(st, k, i)
            first[k, i] = value
            fy[0, k, pl.ds(i, 1), :] = value[ny - 1:]
            fy[1, k, pl.ds(i, 1), :] = value[:1]
            if i == nx - 1:
                fx[0, k] = value
            if i == 0:
                fx[1, k] = value
        return carry

    for load in loads[:3]:
        load.wait()
    lax.fori_loop(0, rows, first_inner, 0)
    first_copies = send((
        (fx.at[0], hx2.at[0]), (fx.at[1], hx2.at[1]), (fy.at[0], hy2.at[0]), (fy.at[1], hy2.at[1]),
    ), sides, 8)

    for load in loads[3:]:
        load.wait()
    for i in range(nx):
        numbers[i] = block_numbers(counts, i, row_index, ny)

    def early_group(i, carry):
        part = pl.ds(i * together, together)
        u = [st[s, part] for s in range(rows)]
        number = numbers[part]
        change = chemistry(u, number, time_step / number, log_rate, activation, heat, 0, most_steps)
        for s in range(rows):
            nxt[s, part] = 0.5 * (u[s] + change[s])
        return carry

    lax.fori_loop(0, nx // together, early_group, 0)

    def first_outer(k, carry):
        weight = time_step * diffusivity[k]
        for i in range(nx):
            first[k, i] = first[k, i] + weight * outer_laplace(hx1, hy1, k, i, at_low, at_high)
        return carry

    for copy in state_copies + corner_copies:
        copy.wait_recv()
    lax.fori_loop(0, rows, first_outer, 0)
    first_store = pltpu.make_async_copy(first, first_out, store_sem.at[0])
    first_store.start()

    def next_inner(k, carry):
        weight = time_step * diffusivity[k]
        corner = [corners[n, pl.ds(k, 1), :] for n in range(4)]
        for i in range(nx):
            here = st[k, i]
            edge = jnp.where(at_low | at_high, here, 0.0)
            if i in (0, nx - 1):
                n = 2 * (i // (nx - 1))
                low = jnp.where(at_low, corner[n], 0.0)
                edge = edge + here + 2.0 * jnp.where(at_high, corner[n + 1], low)
            own = nxt[k, i] + 0.5 * first[k, i]
            nxt[k, i] = own + (0.5 * weight) * (inner_laplace(first, k, i) + weight * edge)
        return carry

    lax.fori_loop(0, rows, next_inner, 0)
    next_store = pltpu.make_async_copy(nxt, next_out, store_sem.at[1])
    next_store.start()
    for copy in first_copies:
        copy.wait_recv()
    for copy in state_copies + corner_copies + first_copies:
        copy.wait_send()
    first_store.wait()
    next_store.wait()


def second_kernel(
    first_in, next_in, hx_in, hy_in, counts_in, diffusivity_in, log_rate_in, activation_in, heat_in,
    next_out, late_out,
    first, nxt, late, hx, hy, counts, diffusivity, log_rate, activation, heat, small_sem, load_sem, next_sem, late_sem,
):
    rows, nx, ny, nz = first.shape
    groups = nx // together
    pairs = (
        (counts_in, counts), (diffusivity_in, diffusivity), (log_rate_in, log_rate), (activation_in, activation),
        (heat_in, heat), (hx_in, hx), (hy_in, hy),
    )
    small = [pltpu.make_async_copy(one, two, small_sem.at[n]) for n, (one, two) in enumerate(pairs)]

    def span(i):
        return pl.ds(i * together, together)

    def first_load(i):
        return pltpu.make_async_copy(first_in.at[:, span(i)], first.at[:, span(i)], load_sem.at[i])

    def late_store(i):
        return pltpu.make_async_copy(late.at[:, span(i)], late_out.at[:, span(i)], late_sem.at[i])

    next_load = pltpu.make_async_copy(next_in, nxt, next_sem.at[0])
    next_store = pltpu.make_async_copy(nxt, next_out, next_sem.at[1])
    for copy in small:
        copy.start()
    next_load.start()
    for i in range(groups):
        first_load(i).start()
    row_index = lax.broadcasted_iota(jnp.int32, (ny, nz), 0)
    at_low, at_high = row_index == 0, row_index == ny - 1

    def next_outer(k, carry):
        weight = (0.5 * time_step) * diffusivity[k]
        for i in range(nx):
            nxt[k, i] = nxt[k, i] + weight * outer_laplace(hx, hy, k, i, at_low, at_high)
        return carry

    for copy in small:
        copy.wait()
    next_load.wait()
    lax.fori_loop(0, rows, next_outer, 0)
    next_store.start()

    def group(i, carry):
        last = counts[i * together, 0]
        for n in range(together):
            for j in range(ny):
                last = jnp.maximum(last, counts[i * together + n, j])
        number = jnp.stack([block_numbers(counts, i * together + n, row_index, ny) for n in range(together)])
        first_load(i).wait()

        def run(upto):
            u = [first[s, span(i)] for s in range(rows)]
            change = chemistry(u, number, time_step / number, log_rate, activation, heat, 0, upto)
            for s in range(rows):
                late[s, span(i)] = change[s] * (1.0 / time_step)

        @pl.when(last <= late_steps)
        def _():
            run(late_steps)

        @pl.when(last > late_steps)
        def _():
            run(most_steps)

        late_store(i).start()
        return carry

    lax.fori_loop(0, groups, group, 0)
    next_store.wait()
    for i in range(groups):
        late_store(i).wait()


def local(state, source_in, counts, diffusivity, log_rate, activation, heat_release):
    rows, nx, ny, nz = state.shape
    whole = jax.ShapeDtypeStruct(state.shape, jnp.float32)
    field = pltpu.VMEM(state.shape, jnp.float32)
    outside = pl.BlockSpec(memory_space=pl.ANY)
    scalars = [pltpu.SMEM(a.shape, a.dtype) for a in (counts, log_rate, activation, heat_release)]
    halo_x = pltpu.VMEM((2, rows, ny, nz), jnp.float32)
    halo_y = pltpu.VMEM((2, rows, nx, nz), jnp.float32)
    wall_x = jax.ShapeDtypeStruct(halo_x.shape, jnp.float32)
    wall_y = jax.ShapeDtypeStruct(halo_y.shape, jnp.float32)
    spread = pltpu.SMEM(diffusivity.shape, jnp.float32)
    first, partial, hx, hy = pl.pallas_call(
        first_kernel,
        out_shape=(whole, whole, wall_x, wall_y),
        in_specs=[outside] * 7,
        out_specs=(outside,) * 4,
        scratch_shapes=[
            field, field, field, field,
            scalars[0], spread, *scalars[1:],
            pltpu.VMEM((nx, ny, nz), jnp.float32),
            halo_x, halo_y, halo_x, halo_y, pltpu.VMEM((4, rows, nz), jnp.float32),
            pltpu.SemaphoreType.DMA((7,)),
            pltpu.SemaphoreType.DMA((2,)),
            pltpu.SemaphoreType.DMA((12,)),
            pltpu.SemaphoreType.DMA((12,)),
        ],
        compiler_params=pltpu.CompilerParams(
            collective_id=0, has_side_effects=True, vmem_limit_bytes=60 * 1024 * 1024,
        ),
        name="sections",
    )(state, source_in, counts, diffusivity, log_rate, activation, heat_release)
    return pl.pallas_call(
        second_kernel,
        out_shape=(whole,) * 2,
        in_specs=[outside] * 9,
        out_specs=(outside,) * 2,
        scratch_shapes=[
            field, field, field, halo_x, halo_y, scalars[0], spread, *scalars[1:],
            pltpu.SemaphoreType.DMA((7,)),
            pltpu.SemaphoreType.DMA((nx // together,)),
            pltpu.SemaphoreType.DMA((2,)),
            pltpu.SemaphoreType.DMA((nx // together,)),
        ],
        compiler_params=pltpu.CompilerParams(vmem_limit_bytes=60 * 1024 * 1024),
        name="finish",
    )(first, partial, hx, hy, counts, diffusivity, log_rate, activation, heat_release)


def solution(mesh):
    grid = P(None, "gx", "gy", None)
    return jax.shard_map(
        local,
        mesh=mesh,
        in_specs=(grid, grid, P("gx", "gy"), P(), P(), P(), P()),
        out_specs=(grid, grid),
        check_vma=False,
    )
```

```python
import jax
import jax.numpy as jnp
import numpy as np
from jax import lax
from jax.experimental import pallas as pl
from jax.experimental.pallas import tpu as pltpu
from jax.sharding import PartitionSpec as P

time_step = 0.15
log2_e = 1.4426950408889634
most_steps = 8
late_steps = 2
together = 2
reaction_table = (
    (3, 1, (4, 5)),
    (4, 0, (3, 5)),
    (5, 0, (3, 2)),
    (5, 5, (4, 2)),
    (3, 3, (0,)),
    (3, 5, (2,)),
    (4, 4, (1,)),
    (3, 4, (5,)),
    (3, 1, (6,)),
    (6, 3, (0, 1)),
    (6, 3, (5, 5)),
    (6, 4, (1, 5)),
    (6, 5, (2, 1)),
    (6, 6, (7, 1)),
    (7, 9, (5, 5)),
    (7, 3, (2, 5)),
    (7, 3, (6, 0)),
    (7, 4, (5, 6)),
    (7, 5, (6, 2)),
    (0, 9, (3, 3)),
    (2, 9, (3, 5)),
)
free_rows = (0, 1, 2, 4, 6, 7)
spanning = (7, 11, 14, 17, 19, 20)


def spanning_tables():
    change = np.zeros((9, 21))
    for reaction, (one, two, products) in enumerate(reaction_table):
        change[one, reaction] -= 1.0
        if two < 9:
            change[two, reaction] -= 1.0
        for product in products:
            change[product, reaction] += 1.0
    kept = change[list(free_rows)]
    inverse = np.round(np.linalg.inv(kept[:, list(spanning)]), 6)
    return inverse, np.round(inverse @ kept, 6)


def weighted(terms):
    total = None
    for weight, value in terms:
        if weight == 0:
            continue
        term = value if weight == 1 else value * float(weight)
        total = term if total is None else total + term
    return total


def heat_scalars(heat):
    inverse, spans = spanning_tables()
    base = [heat[r] for r in spanning]
    on_rows = [weighted([(inverse[i, j], base[i]) for i in range(6)]) for j in range(6)]
    on_reactions = {}
    for r in range(21):
        if r not in spanning:
            on_reactions[r] = weighted([(1.0, heat[r])] + [(-spans[i, r], base[i]) for i in range(6)])
    return on_rows, on_reactions


def prepare(temperature, stride, log_rate, activation):
    inverse_t = 1.0 / temperature
    return [jnp.exp2(log_rate[r] * log2_e - (activation[r] * log2_e) * inverse_t) * stride for r in range(21)]


def atoms(u):
    h2, o2, h2o, h, o, oh, ho2, h2o2 = u
    oxygen = 2.0 * (o2 + ho2 + h2o2) + h2o + o + oh
    surplus = 2.0 * (h2 - o2) + h2o + h - ho2 - o
    return oxygen, surplus


def substep(u, kept, k, active):
    h2, o2, h2o, h, o, oh, ho2, h2o2 = u
    oxygen, surplus = kept
    a, b, c, d, e, f, g = (h2, h2o, h, o, oh, ho2, h2o2)
    if active is not None:
        a, b, c, d, e, f, g = [jnp.where(active, v, 0.0) for v in (a, b, c, d, e, f, g)]
    p = {0: c * o2, 1: d * a, 2: e * a, 3: e * e, 4: c * c, 5: c * e, 6: d * d, 9: f * c, 12: f * e, 13: f * f,
         15: g * c, 18: g * e}
    w = {r: k[r] * v for r, v in p.items()}
    w[8] = k[8] * p[0]
    w[10] = k[10] * p[9]
    w[16] = k[16] * p[15]
    w[7] = k[7] * (c * d)
    w[11] = k[11] * (f * d)
    w[17] = k[17] * (g * d)
    w[14] = k[14] * g
    w[19] = k[19] * a
    w[20] = k[20] * b
    s1 = w[16] + w[17] + w[18]
    s2 = (w[9] + w[13]) + (w[11] + w[12])
    h2 = h2 + (((w[4] + w[9]) + (w[16] - w[1])) - (w[2] + w[19]))
    o2 = o2 + ((s2 + w[6]) - (w[0] + w[8]))
    h2o = h2o + (((w[2] + w[3]) + (w[5] + w[12])) + ((w[15] + w[18]) - w[20]))
    o = o + (((w[0] + w[3]) - (w[1] + w[7])) - ((w[6] + w[6]) + (w[11] + w[17])))
    ho2 = ho2 + (((s1 + w[8]) - s2) - (w[10] + w[13]))
    h2o2 = h2o2 + ((w[13] - s1) - (w[14] + w[15]))
    oh = ((oxygen - h2o) - o) - 2.0 * ((o2 + ho2) + h2o2)
    h = ((surplus - h2o) + (ho2 + o)) - 2.0 * (h2 - o2)
    return (h2, o2, h2o, h, o, oh, ho2, h2o2), p


def warmth(change, sums, k, heat):
    on_rows, on_reactions = heat_scalars(heat)
    rate = {r: on_reactions[r] * k[r] for r in on_reactions}
    rate[0] = rate[0] + rate.pop(8)
    rate[9] = rate[9] + rate.pop(10)
    rate[15] = rate[15] + rate.pop(16)
    terms = [rate[r] * total for r, total in sums.items()]
    terms += [weight * change[row] for weight, row in zip(on_rows, free_rows)]
    while len(terms) > 1:
        terms = [sum(terms[i + 1:i + 2], terms[i]) for i in range(0, len(terms), 2)]
    return terms[0]


def chemistry(u, counts, stride, log_rate, activation, heat, done, upto):
    k = prepare(u[9], stride, log_rate, activation)
    before = tuple(u[:8])
    kept = atoms(before)
    now, sums = before, None
    for turn in range(done, upto):
        now, p = substep(now, kept, k, None if turn == 0 else counts > float(turn))
        sums = p if sums is None else {r: sums[r] + p[r] for r in sums}
    change = [after - start for after, start in zip(now, before)]
    return change + [jnp.zeros_like(u[9]), warmth(change, sums, k, heat)]


def block_numbers(counts, i, row_index, ny):
    number = jnp.zeros(row_index.shape, jnp.int32)
    for j in range(ny):
        number = jnp.where(row_index == j, counts[i, j], number)
    return number.astype(jnp.float32)


def first_kernel(
    state, source, counts_in, diffusivity_in, log_rate_in, activation_in, heat_in,
    first_out, next_out,
    st, src, first, nxt, counts, diffusivity, log_rate, activation, heat, numbers,
    own_x, own_y, own_corners, fx, fy, hx1, hy1, corners, hx2, hy2,
    load_sem, store_sem, send_sem, recv_sem,
):
    rows, nx, ny, nz = st.shape
    x, size_x = lax.axis_index("gx"), lax.axis_size("gx")
    y, size_y = lax.axis_index("gy"), lax.axis_size("gy")
    x_up, x_down = lax.rem(x + 1, size_x), lax.rem(x + size_x - 1, size_x)
    y_up, y_down = lax.rem(y + 1, size_y), lax.rem(y + size_y - 1, size_y)
    sides = ((x_up, y), (x_down, y), (x, y_up), (x, y_down))
    diagonals = ((x_up, y_up), (x_up, y_down), (x_down, y_up), (x_down, y_down))
    barrier = pltpu.get_barrier_semaphore()
    for device in diagonals + sides:
        pl.semaphore_signal(barrier, inc=1, device_id=device, device_id_type=pl.DeviceIdType.MESH)
    pairs = (
        (state, st), (source, src), (diffusivity_in, diffusivity),
        (counts_in, counts), (log_rate_in, log_rate), (activation_in, activation), (heat_in, heat),
    )
    loads = [pltpu.make_async_copy(one, two, load_sem.at[n]) for n, (one, two) in enumerate(pairs)]
    for load in loads:
        load.start()

    def send(pieces, devices, base):
        copies = []
        for place, (piece, device) in enumerate(zip(pieces, devices)):
            copies.append(pltpu.make_async_remote_copy(
                src_ref=piece[0], dst_ref=piece[1],
                send_sem=send_sem.at[base + place], recv_sem=recv_sem.at[base + place],
                device_id=device, device_id_type=pl.DeviceIdType.MESH,
            ))
        for copy in copies[::-1]:
            copy.start()
        return copies

    def pack(k, carry):
        for i in range(nx):
            value = st[k, i]
            own_y[0, k, pl.ds(i, 1), :] = value[ny - 1:]
            own_y[1, k, pl.ds(i, 1), :] = value[:1]
            if i in (0, nx - 1):
                n = 0 if i == nx - 1 else 1
                own_x[n, k] = value
                own_corners[2 * n, k] = value[ny - 1:]
                own_corners[2 * n + 1, k] = value[:1]
        return carry

    loads[0].wait()
    lax.fori_loop(0, rows, pack, 0)
    pl.semaphore_wait(barrier, 8)
    state_copies = send((
        (own_x.at[0], hx1.at[0]), (own_x.at[1], hx1.at[1]), (own_y.at[0], hy1.at[0]), (own_y.at[1], hy1.at[1]),
    ), sides, 0)
    corner_copies = send(tuple((own_corners.at[n], corners.at[n]) for n in range(4)), diagonals, 4)

    row_index = lax.broadcasted_iota(jnp.int32, (ny, nz), 0)
    at_low, at_high = row_index == 0, row_index == ny - 1

    def inner_laplace(field, k, i):
        here = field[k, i]
        low = jnp.where(at_low, 0.0, pltpu.roll(here, 1, 0))
        high = jnp.where(at_high, 0.0, pltpu.roll(here, ny - 1, 0))
        beside = (low + high) + (pltpu.roll(here, 1, 1) + pltpu.roll(here, nz - 1, 1))
        if i > 0:
            beside = beside + field[k, i - 1]
        if i < nx - 1:
            beside = beside + field[k, i + 1]
        return beside - 6.0 * here

    def outer_laplace(halo_x, halo_y, k, i):
        low = jnp.where(at_low, halo_y[0, k, pl.ds(i, 1), :], 0.0)
        rest = jnp.where(at_high, halo_y[1, k, pl.ds(i, 1), :], low)
        if i == 0:
            rest = rest + halo_x[0, k]
        if i == nx - 1:
            rest = rest + halo_x[1, k]
        return rest

    def first_inner(k, carry):
        weight = time_step * diffusivity[k]
        for i in range(nx):
            value = (st[k, i] + time_step * src[k, i]) + weight * inner_laplace(st, k, i)
            first[k, i] = value
            fy[0, k, pl.ds(i, 1), :] = value[ny - 1:]
            fy[1, k, pl.ds(i, 1), :] = value[:1]
            if i == nx - 1:
                fx[0, k] = value
            if i == 0:
                fx[1, k] = value
        return carry

    for load in loads[1:3]:
        load.wait()
    lax.fori_loop(0, rows, first_inner, 0)
    first_copies = send((
        (fx.at[0], hx2.at[0]), (fx.at[1], hx2.at[1]), (fy.at[0], hy2.at[0]), (fy.at[1], hy2.at[1]),
    ), sides, 8)

    for load in loads[3:]:
        load.wait()
    for i in range(nx):
        numbers[i] = block_numbers(counts, i, row_index, ny)

    def early_group(i, carry):
        part = pl.ds(i * together, together)
        u = [st[s, part] for s in range(rows)]
        number = numbers[part]
        change = chemistry(u, number, time_step / number, log_rate, activation, heat, 0, most_steps)
        for s in range(rows):
            nxt[s, part] = 0.5 * (u[s] + change[s])
        return carry

    lax.fori_loop(0, nx // together, early_group, 0)

    def first_outer(k, carry):
        weight = time_step * diffusivity[k]
        for i in range(nx):
            first[k, i] = first[k, i] + weight * outer_laplace(hx1, hy1, k, i)
        return carry

    for copy in state_copies:
        copy.wait_recv()
    lax.fori_loop(0, rows, first_outer, 0)
    first_store = pltpu.make_async_copy(first, first_out, store_sem.at[0])
    first_store.start()

    def next_inner(k, carry):
        weight = (0.5 * time_step) * diffusivity[k]
        for i in range(nx):
            nxt[k, i] = (nxt[k, i] + 0.5 * first[k, i]) + weight * inner_laplace(first, k, i)
        return carry

    lax.fori_loop(0, rows, next_inner, 0)
    for copy in corner_copies + first_copies:
        copy.wait_recv()

    side_index = lax.broadcasted_iota(jnp.int32, (nx, nz), 0)

    def next_outer(k, carry):
        weight = time_step * diffusivity[k]
        corner = [corners[n, k] for n in range(4)]
        for n, plane in ((0, st[k, 0]), (1, st[k, nx - 1])):
            low = jnp.where(at_low, corner[2 * n], 0.0)
            rest = jnp.where(at_high, corner[2 * n + 1], low)
            hx2[n, k] = hx2[n, k] + weight * (plane + rest)
        for n in range(2):
            low = jnp.where(side_index == 0, corner[n], 0.0)
            rest = jnp.where(side_index == nx - 1, corner[2 + n], low)
            hy2[n, k] = hy2[n, k] + weight * (own_y[1 - n, k] + rest)
        for i in range(nx):
            nxt[k, i] = nxt[k, i] + (0.5 * weight) * outer_laplace(hx2, hy2, k, i)
        return carry

    half = rows // 2
    stores = [first_store]
    for n in range(2):
        lax.fori_loop(n * half, n * half + half, next_outer, 0)
        part = pl.ds(n * half, half)
        stores.append(pltpu.make_async_copy(nxt.at[part], next_out.at[part], store_sem.at[1 + n]))
        stores[-1].start()
    for copy in state_copies + corner_copies + first_copies:
        copy.wait_send()
    for store in stores:
        store.wait()


def second_kernel(
    first_in, next_in, counts_in, log_rate_in, activation_in, heat_in,
    next_out, late_out,
    first, nxt, late, counts, log_rate, activation, heat, small_sem, load_sem, next_sem, late_sem,
):
    rows, nx, ny, nz = first.shape
    groups = nx // together
    pairs = ((counts_in, counts), (log_rate_in, log_rate), (activation_in, activation), (heat_in, heat))
    small = [pltpu.make_async_copy(one, two, small_sem.at[n]) for n, (one, two) in enumerate(pairs)]

    def span(i):
        return pl.ds(i * together, together)

    def first_load(i):
        return pltpu.make_async_copy(first_in.at[:, span(i)], first.at[:, span(i)], load_sem.at[i])

    def late_store(i):
        return pltpu.make_async_copy(late.at[:, span(i)], late_out.at[:, span(i)], late_sem.at[i])

    next_load = pltpu.make_async_copy(next_in, nxt, next_sem.at[0])
    next_store = pltpu.make_async_copy(nxt, next_out, next_sem.at[1])
    for copy in small:
        copy.start()
    for i in range(groups):
        first_load(i).start()
    next_load.start()
    for copy in small:
        copy.wait()
    row_index = lax.broadcasted_iota(jnp.int32, (ny, nz), 0)

    def group(i, carry):
        last = counts[i * together, 0]
        for n in range(together):
            for j in range(ny):
                last = jnp.maximum(last, counts[i * together + n, j])
        number = jnp.stack([block_numbers(counts, i * together + n, row_index, ny) for n in range(together)])
        first_load(i).wait()

        def run(upto):
            u = [first[s, span(i)] for s in range(rows)]
            change = chemistry(u, number, time_step / number, log_rate, activation, heat, 0, upto)
            for s in range(rows):
                late[s, span(i)] = change[s] * (1.0 / time_step)

        @pl.when(last <= late_steps)
        def _():
            run(late_steps)

        @pl.when(last > late_steps)
        def _():
            run(most_steps)

        late_store(i).start()

        @pl.when(i == 0)
        def _():
            next_load.wait()
            next_store.start()

        return carry

    lax.fori_loop(0, groups, group, 0)
    next_store.wait()
    for i in range(groups):
        late_store(i).wait()


def local(state, source_in, counts, diffusivity, log_rate, activation, heat_release):
    rows, nx, ny, nz = state.shape
    whole = jax.ShapeDtypeStruct(state.shape, jnp.float32)
    field = pltpu.VMEM(state.shape, jnp.float32)
    outside = pl.BlockSpec(memory_space=pl.ANY)
    scalars = [pltpu.SMEM(a.shape, a.dtype) for a in (counts, log_rate, activation, heat_release)]
    halo_x = pltpu.VMEM((2, rows, ny, nz), jnp.float32)
    corner = pltpu.VMEM((4, rows, 1, nz), jnp.float32)
    halo_y = pltpu.VMEM((2, rows, nx, nz), jnp.float32)
    first, partial = pl.pallas_call(
        first_kernel,
        out_shape=(whole,) * 2,
        in_specs=[outside] * 7,
        out_specs=(outside,) * 2,
        scratch_shapes=[
            field, field, field, field,
            scalars[0], pltpu.SMEM(diffusivity.shape, jnp.float32), *scalars[1:],
            pltpu.VMEM((nx, ny, nz), jnp.float32),
            halo_x, halo_y, corner, halo_x, halo_y, halo_x, halo_y, corner, halo_x, halo_y,
            pltpu.SemaphoreType.DMA((7,)),
            pltpu.SemaphoreType.DMA((3,)),
            pltpu.SemaphoreType.DMA((12,)),
            pltpu.SemaphoreType.DMA((12,)),
        ],
        compiler_params=pltpu.CompilerParams(
            collective_id=0, has_side_effects=True, vmem_limit_bytes=60 * 1024 * 1024,
        ),
        name="sections",
    )(state, source_in, counts, diffusivity, log_rate, activation, heat_release)
    return pl.pallas_call(
        second_kernel,
        out_shape=(whole,) * 2,
        in_specs=[outside] * 6,
        out_specs=(outside,) * 2,
        scratch_shapes=[
            field, field, field, *scalars,
            pltpu.SemaphoreType.DMA((4,)),
            pltpu.SemaphoreType.DMA((nx // together,)),
            pltpu.SemaphoreType.DMA((2,)),
            pltpu.SemaphoreType.DMA((nx // together,)),
        ],
        compiler_params=pltpu.CompilerParams(vmem_limit_bytes=60 * 1024 * 1024),
        name="finish",
    )(first, partial, counts, log_rate, activation, heat_release)


def solution(mesh):
    grid = P(None, "gx", "gy", None)
    return jax.shard_map(
        local,
        mesh=mesh,
        in_specs=(grid, grid, P("gx", "gy"), P(), P(), P(), P()),
        out_specs=(grid, grid),
        check_vma=False,
    )
```

```python
import jax
import jax.numpy as jnp
import numpy as np
from jax import lax
from jax.experimental import pallas as pl
from jax.experimental.pallas import tpu as pltpu
from jax.sharding import PartitionSpec as P

time_step = 0.15
log2_e = 1.4426950408889634
most_steps = 8
together = 2
reaction_table = (
    (3, 1, (4, 5)),
    (4, 0, (3, 5)),
    (5, 0, (3, 2)),
    (5, 5, (4, 2)),
    (3, 3, (0,)),
    (3, 5, (2,)),
    (4, 4, (1,)),
    (3, 4, (5,)),
    (3, 1, (6,)),
    (6, 3, (0, 1)),
    (6, 3, (5, 5)),
    (6, 4, (1, 5)),
    (6, 5, (2, 1)),
    (6, 6, (7, 1)),
    (7, 9, (5, 5)),
    (7, 3, (2, 5)),
    (7, 3, (6, 0)),
    (7, 4, (5, 6)),
    (7, 5, (6, 2)),
    (0, 9, (3, 3)),
    (2, 9, (3, 5)),
)
free_rows = (0, 1, 2, 4, 6, 7)
spanning = (7, 11, 14, 17, 19, 20)


def spanning_tables():
    change = np.zeros((9, 21))
    for reaction, (one, two, products) in enumerate(reaction_table):
        change[one, reaction] -= 1.0
        if two < 9:
            change[two, reaction] -= 1.0
        for product in products:
            change[product, reaction] += 1.0
    kept = change[list(free_rows)]
    inverse = np.round(np.linalg.inv(kept[:, list(spanning)]), 6)
    return inverse, np.round(inverse @ kept, 6)


def weighted(terms):
    total = None
    for weight, value in terms:
        if weight == 0:
            continue
        term = value if weight == 1 else value * float(weight)
        total = term if total is None else total + term
    return total


def heat_scalars(heat):
    inverse, spans = spanning_tables()
    base = [heat[r] for r in spanning]
    on_rows = [weighted([(inverse[i, j], base[i]) for i in range(6)]) for j in range(6)]
    on_reactions = {}
    for r in range(21):
        if r not in spanning:
            on_reactions[r] = weighted([(1.0, heat[r])] + [(-spans[i, r], base[i]) for i in range(6)])
    return on_rows, on_reactions


def prepare(temperature, stride, log_rate, activation):
    inverse_t = 1.0 / temperature
    return [jnp.exp2(log_rate[r] * log2_e - (activation[r] * log2_e) * inverse_t) * stride for r in range(21)]


def atoms(u):
    h2, o2, h2o, h, o, oh, ho2, h2o2 = u
    oxygen = 2.0 * (o2 + ho2 + h2o2) + h2o + o + oh
    surplus = 2.0 * (h2 - o2) + h2o + h - ho2 - o
    return oxygen, surplus


def substep(u, kept, k, active):
    h2, o2, h2o, h, o, oh, ho2, h2o2 = u
    oxygen, surplus = kept
    a, b, c, d, e, f, g = (h2, h2o, h, o, oh, ho2, h2o2)
    if active is not None:
        a, b, c, d, e, f, g = [jnp.where(active, v, 0.0) for v in (a, b, c, d, e, f, g)]
    p = {0: c * o2, 1: d * a, 2: e * a, 3: e * e, 4: c * c, 5: c * e, 6: d * d, 9: f * c, 12: f * e, 13: f * f,
         15: g * c, 18: g * e}
    w = {r: k[r] * v for r, v in p.items()}
    w[8] = k[8] * p[0]
    w[10] = k[10] * p[9]
    w[16] = k[16] * p[15]
    w[7] = k[7] * (c * d)
    w[11] = k[11] * (f * d)
    w[17] = k[17] * (g * d)
    w[14] = k[14] * g
    w[19] = k[19] * a
    w[20] = k[20] * b
    s1 = w[16] + w[17] + w[18]
    s2 = (w[9] + w[13]) + (w[11] + w[12])
    h2 = h2 + (((w[4] + w[9]) + (w[16] - w[1])) - (w[2] + w[19]))
    o2 = o2 + ((s2 + w[6]) - (w[0] + w[8]))
    h2o = h2o + (((w[2] + w[3]) + (w[5] + w[12])) + ((w[15] + w[18]) - w[20]))
    o = o + (((w[0] + w[3]) - (w[1] + w[7])) - ((w[6] + w[6]) + (w[11] + w[17])))
    ho2 = ho2 + (((s1 + w[8]) - s2) - (w[10] + w[13]))
    h2o2 = h2o2 + ((w[13] - s1) - (w[14] + w[15]))
    oh = ((oxygen - h2o) - o) - 2.0 * ((o2 + ho2) + h2o2)
    h = ((surplus - h2o) + (ho2 + o)) - 2.0 * (h2 - o2)
    return (h2, o2, h2o, h, o, oh, ho2, h2o2), p


def warmth(change, sums, k, heat):
    on_rows, on_reactions = heat_scalars(heat)
    rate = {r: on_reactions[r] * k[r] for r in on_reactions}
    rate[0] = rate[0] + rate.pop(8)
    rate[9] = rate[9] + rate.pop(10)
    rate[15] = rate[15] + rate.pop(16)
    terms = [rate[r] * total for r, total in sums.items()]
    terms += [weight * change[row] for weight, row in zip(on_rows, free_rows)]
    while len(terms) > 1:
        terms = [sum(terms[i + 1:i + 2], terms[i]) for i in range(0, len(terms), 2)]
    return terms[0]


def chemistry(u, counts, stride, log_rate, activation, heat, done, upto):
    k = prepare(u[9], stride, log_rate, activation)
    before = tuple(u[:8])
    kept = atoms(before)
    now, sums = before, None
    for turn in range(done, upto):
        now, p = substep(now, kept, k, None if turn == 0 else counts > float(turn))
        sums = p if sums is None else {r: sums[r] + p[r] for r in sums}
    change = [after - start for after, start in zip(now, before)]
    return change + [jnp.zeros_like(u[9]), warmth(change, sums, k, heat)]


def block_numbers(counts, i, row_index, ny):
    number = jnp.zeros(row_index.shape, jnp.int32)
    for j in range(ny):
        number = jnp.where(row_index == j, counts[i, j], number)
    return number.astype(jnp.float32)


def first_kernel(
    state, source, counts_in, diffusivity_in, log_rate_in, activation_in, heat_in,
    late_out, next_out,
    st, src, first, nxt, late, counts, diffusivity, log_rate, activation, heat, numbers,
    own_x, own_y, own_corners, fx, fy, hx1, hy1, corners, hx2, hy2,
    load_sem, store_sem, send_sem, recv_sem,
):
    rows, nx, ny, nz = st.shape
    x, size_x = lax.axis_index("gx"), lax.axis_size("gx")
    y, size_y = lax.axis_index("gy"), lax.axis_size("gy")
    x_up, x_down = lax.rem(x + 1, size_x), lax.rem(x + size_x - 1, size_x)
    y_up, y_down = lax.rem(y + 1, size_y), lax.rem(y + size_y - 1, size_y)
    sides = ((x_up, y), (x_down, y), (x, y_up), (x, y_down))
    diagonals = ((x_up, y_up), (x_up, y_down), (x_down, y_up), (x_down, y_down))
    barrier = pltpu.get_barrier_semaphore()
    for device in diagonals + sides:
        pl.semaphore_signal(barrier, inc=1, device_id=device, device_id_type=pl.DeviceIdType.MESH)
    pairs = (
        (state, st), (source, src), (diffusivity_in, diffusivity),
        (counts_in, counts), (log_rate_in, log_rate), (activation_in, activation), (heat_in, heat),
    )
    loads = [pltpu.make_async_copy(one, two, load_sem.at[n]) for n, (one, two) in enumerate(pairs)]
    for load in loads:
        load.start()

    def send(pieces, devices, base):
        copies = []
        for place, (piece, device) in enumerate(zip(pieces, devices)):
            copies.append(pltpu.make_async_remote_copy(
                src_ref=piece[0], dst_ref=piece[1],
                send_sem=send_sem.at[base + place], recv_sem=recv_sem.at[base + place],
                device_id=device, device_id_type=pl.DeviceIdType.MESH,
            ))
        for copy in copies[::-1]:
            copy.start()
        return copies

    def pack(k, carry):
        for i in range(nx):
            value = st[k, i]
            own_y[0, k, pl.ds(i, 1), :] = value[ny - 1:]
            own_y[1, k, pl.ds(i, 1), :] = value[:1]
            if i in (0, nx - 1):
                n = 0 if i == nx - 1 else 1
                own_x[n, k] = value
                own_corners[2 * n, k] = value[ny - 1:]
                own_corners[2 * n + 1, k] = value[:1]
        return carry

    loads[0].wait()
    lax.fori_loop(0, rows, pack, 0)
    pl.semaphore_wait(barrier, 8)
    state_copies = send((
        (own_x.at[0], hx1.at[0]), (own_x.at[1], hx1.at[1]), (own_y.at[0], hy1.at[0]), (own_y.at[1], hy1.at[1]),
    ), sides, 0)
    corner_copies = send(tuple((own_corners.at[n], corners.at[n]) for n in range(4)), diagonals, 4)

    row_index = lax.broadcasted_iota(jnp.int32, (ny, nz), 0)
    at_low, at_high = row_index == 0, row_index == ny - 1

    def inner_laplace(field, k, i):
        here = field[k, i]
        low = jnp.where(at_low, 0.0, pltpu.roll(here, 1, 0))
        high = jnp.where(at_high, 0.0, pltpu.roll(here, ny - 1, 0))
        beside = (low + high) + (pltpu.roll(here, 1, 1) + pltpu.roll(here, nz - 1, 1))
        if i > 0:
            beside = beside + field[k, i - 1]
        if i < nx - 1:
            beside = beside + field[k, i + 1]
        return beside - 6.0 * here

    def outer_laplace(halo_x, halo_y, k, i):
        low = jnp.where(at_low, halo_y[0, k, pl.ds(i, 1), :], 0.0)
        rest = jnp.where(at_high, halo_y[1, k, pl.ds(i, 1), :], low)
        if i == 0:
            rest = rest + halo_x[0, k]
        if i == nx - 1:
            rest = rest + halo_x[1, k]
        return rest

    def first_inner(k, carry):
        weight = time_step * diffusivity[k]
        for i in range(nx):
            value = (st[k, i] + time_step * src[k, i]) + weight * inner_laplace(st, k, i)
            first[k, i] = value
            fy[0, k, pl.ds(i, 1), :] = value[ny - 1:]
            fy[1, k, pl.ds(i, 1), :] = value[:1]
            if i == nx - 1:
                fx[0, k] = value
            if i == 0:
                fx[1, k] = value
        return carry

    for load in loads[1:3]:
        load.wait()
    lax.fori_loop(0, rows, first_inner, 0)
    first_copies = send((
        (fx.at[0], hx2.at[0]), (fx.at[1], hx2.at[1]), (fy.at[0], hy2.at[0]), (fy.at[1], hy2.at[1]),
    ), sides, 8)

    for load in loads[3:]:
        load.wait()
    for i in range(nx):
        numbers[i] = block_numbers(counts, i, row_index, ny)

    def early_group(i, carry):
        part = pl.ds(i * together, together)
        u = [st[s, part] for s in range(rows)]
        number = numbers[part]
        change = chemistry(u, number, time_step / number, log_rate, activation, heat, 0, most_steps)
        for s in range(rows):
            nxt[s, part] = 0.5 * (u[s] + change[s])
        return carry

    lax.fori_loop(0, nx // together, early_group, 0)

    def first_outer(k, carry):
        weight = time_step * diffusivity[k]
        for i in range(nx):
            first[k, i] = first[k, i] + weight * outer_laplace(hx1, hy1, k, i)
        return carry

    for copy in state_copies:
        copy.wait_recv()
    lax.fori_loop(0, rows, first_outer, 0)

    def next_inner(k, carry):
        weight = (0.5 * time_step) * diffusivity[k]
        for i in range(nx):
            nxt[k, i] = (nxt[k, i] + 0.5 * first[k, i]) + weight * inner_laplace(first, k, i)
        return carry

    lax.fori_loop(0, rows, next_inner, 0)

    def late_group(i, carry):
        part = pl.ds(i * together, together)
        u = [first[s, part] for s in range(rows)]
        number = numbers[part]
        change = chemistry(u, number, time_step / number, log_rate, activation, heat, 0, most_steps)
        for s in range(rows):
            late[s, part] = change[s] * (1.0 / time_step)
        return carry

    lax.fori_loop(0, nx // together, late_group, 0)
    late_store = pltpu.make_async_copy(late, late_out, store_sem.at[0])
    late_store.start()
    for copy in corner_copies + first_copies:
        copy.wait_recv()

    side_index = lax.broadcasted_iota(jnp.int32, (nx, nz), 0)

    def next_outer(k, carry):
        weight = time_step * diffusivity[k]
        corner = [corners[n, k] for n in range(4)]
        for n, plane in ((0, st[k, 0]), (1, st[k, nx - 1])):
            low = jnp.where(at_low, corner[2 * n], 0.0)
            rest = jnp.where(at_high, corner[2 * n + 1], low)
            hx2[n, k] = hx2[n, k] + weight * (plane + rest)
        for n in range(2):
            low = jnp.where(side_index == 0, corner[n], 0.0)
            rest = jnp.where(side_index == nx - 1, corner[2 + n], low)
            hy2[n, k] = hy2[n, k] + weight * (own_y[1 - n, k] + rest)
        for i in range(nx):
            nxt[k, i] = nxt[k, i] + (0.5 * weight) * outer_laplace(hx2, hy2, k, i)
        return carry

    half = rows // 2
    stores = [late_store]
    for n in range(2):
        lax.fori_loop(n * half, n * half + half, next_outer, 0)
        part = pl.ds(n * half, half)
        stores.append(pltpu.make_async_copy(nxt.at[part], next_out.at[part], store_sem.at[1 + n]))
        stores[-1].start()
    for copy in state_copies + corner_copies + first_copies:
        copy.wait_send()
    for store in stores:
        store.wait()


def second_kernel(late_in, next_in, next_out, late_out, late, nxt, load_sem, store_sem):
    pieces = [
        (field, one, two, held, pl.ds(2 * n, 2))
        for n in range(late.shape[0] // 2)
        for field, one, two, held in ((0, late_in, late_out, late), (1, next_in, next_out, nxt))
    ]
    loads = [
        pltpu.make_async_copy(one.at[span], held.at[span], load_sem.at[n])
        for n, (field, one, two, held, span) in enumerate(pieces)
    ]
    stores = [
        pltpu.make_async_copy(held.at[span], two.at[span], store_sem.at[n])
        for n, (field, one, two, held, span) in enumerate(pieces)
    ]
    for load in loads:
        load.start()
    for load, store in zip(loads, stores):
        load.wait()
        store.start()
    for store in stores:
        store.wait()


def local(state, source_in, counts, diffusivity, log_rate, activation, heat_release):
    rows, nx, ny, nz = state.shape
    whole = jax.ShapeDtypeStruct(state.shape, jnp.float32)
    field = pltpu.VMEM(state.shape, jnp.float32)
    outside = pl.BlockSpec(memory_space=pl.ANY)
    scalars = [pltpu.SMEM(a.shape, a.dtype) for a in (counts, log_rate, activation, heat_release)]
    halo_x = pltpu.VMEM((2, rows, ny, nz), jnp.float32)
    corner = pltpu.VMEM((4, rows, 1, nz), jnp.float32)
    halo_y = pltpu.VMEM((2, rows, nx, nz), jnp.float32)
    late, partial = pl.pallas_call(
        first_kernel,
        out_shape=(whole,) * 2,
        in_specs=[outside] * 7,
        out_specs=(outside,) * 2,
        scratch_shapes=[
            field, field, field, field, field,
            scalars[0], pltpu.SMEM(diffusivity.shape, jnp.float32), *scalars[1:],
            pltpu.VMEM((nx, ny, nz), jnp.float32),
            halo_x, halo_y, corner, halo_x, halo_y, halo_x, halo_y, corner, halo_x, halo_y,
            pltpu.SemaphoreType.DMA((7,)),
            pltpu.SemaphoreType.DMA((3,)),
            pltpu.SemaphoreType.DMA((12,)),
            pltpu.SemaphoreType.DMA((12,)),
        ],
        compiler_params=pltpu.CompilerParams(
            collective_id=0, has_side_effects=True, vmem_limit_bytes=60 * 1024 * 1024,
        ),
        name="sections",
    )(state, source_in, counts, diffusivity, log_rate, activation, heat_release)
    return pl.pallas_call(
        second_kernel,
        out_shape=(whole,) * 2,
        in_specs=[outside] * 2,
        out_specs=(outside,) * 2,
        scratch_shapes=[
            field, field,
            pltpu.SemaphoreType.DMA((rows // 2 * 2,)),
            pltpu.SemaphoreType.DMA((rows // 2 * 2,)),
        ],
        compiler_params=pltpu.CompilerParams(vmem_limit_bytes=60 * 1024 * 1024),
        name="finish",
    )(late, partial)


def solution(mesh):
    grid = P(None, "gx", "gy", None)
    return jax.shard_map(
        local,
        mesh=mesh,
        in_specs=(grid, grid, P("gx", "gy"), P(), P(), P(), P()),
        out_specs=(grid, grid),
        check_vma=False,
    )
```

```python
import jax
import jax.numpy as jnp
import numpy as np
from jax import lax
from jax.experimental import pallas as pl
from jax.experimental.pallas import tpu as pltpu
from jax.sharding import PartitionSpec as P

time_step = 0.15
log2_e = 1.4426950408889634
most_steps = 8
late_steps = 2
together = 2
reaction_table = (
    (3, 1, (4, 5)),
    (4, 0, (3, 5)),
    (5, 0, (3, 2)),
    (5, 5, (4, 2)),
    (3, 3, (0,)),
    (3, 5, (2,)),
    (4, 4, (1,)),
    (3, 4, (5,)),
    (3, 1, (6,)),
    (6, 3, (0, 1)),
    (6, 3, (5, 5)),
    (6, 4, (1, 5)),
    (6, 5, (2, 1)),
    (6, 6, (7, 1)),
    (7, 9, (5, 5)),
    (7, 3, (2, 5)),
    (7, 3, (6, 0)),
    (7, 4, (5, 6)),
    (7, 5, (6, 2)),
    (0, 9, (3, 3)),
    (2, 9, (3, 5)),
)
free_rows = (0, 1, 2, 4, 6, 7)
spanning = (7, 11, 14, 17, 19, 20)


def spanning_tables():
    change = np.zeros((9, 21))
    for reaction, (one, two, products) in enumerate(reaction_table):
        change[one, reaction] -= 1.0
        if two < 9:
            change[two, reaction] -= 1.0
        for product in products:
            change[product, reaction] += 1.0
    kept = change[list(free_rows)]
    inverse = np.round(np.linalg.inv(kept[:, list(spanning)]), 6)
    return inverse, np.round(inverse @ kept, 6)


def weighted(terms):
    total = None
    for weight, value in terms:
        if weight == 0:
            continue
        term = value if weight == 1 else value * float(weight)
        total = term if total is None else total + term
    return total


def heat_scalars(heat):
    inverse, spans = spanning_tables()
    base = [heat[r] for r in spanning]
    on_rows = [weighted([(inverse[i, j], base[i]) for i in range(6)]) for j in range(6)]
    on_reactions = {}
    for r in range(21):
        if r not in spanning:
            on_reactions[r] = weighted([(1.0, heat[r])] + [(-spans[i, r], base[i]) for i in range(6)])
    return on_rows, on_reactions


def prepare(temperature, stride, log_rate, activation):
    inverse_t = 1.0 / temperature
    return [jnp.exp2(log_rate[r] * log2_e - (activation[r] * log2_e) * inverse_t) * stride for r in range(21)]


def atoms(u):
    h2, o2, h2o, h, o, oh, ho2, h2o2 = u
    oxygen = 2.0 * (o2 + ho2 + h2o2) + h2o + o + oh
    surplus = 2.0 * (h2 - o2) + h2o + h - ho2 - o
    return oxygen, surplus


def substep(u, kept, k, active):
    h2, o2, h2o, h, o, oh, ho2, h2o2 = u
    oxygen, surplus = kept
    a, b, c, d, e, f, g = (h2, h2o, h, o, oh, ho2, h2o2)
    if active is not None:
        a, b, c, d, e, f, g = [jnp.where(active, v, 0.0) for v in (a, b, c, d, e, f, g)]
    p = {0: c * o2, 1: d * a, 2: e * a, 3: e * e, 4: c * c, 5: c * e, 6: d * d, 9: f * c, 12: f * e, 13: f * f,
         15: g * c, 18: g * e}
    w = {r: k[r] * v for r, v in p.items()}
    w[8] = k[8] * p[0]
    w[10] = k[10] * p[9]
    w[16] = k[16] * p[15]
    w[7] = k[7] * (c * d)
    w[11] = k[11] * (f * d)
    w[17] = k[17] * (g * d)
    w[14] = k[14] * g
    w[19] = k[19] * a
    w[20] = k[20] * b
    s1 = w[16] + w[17] + w[18]
    s2 = (w[9] + w[13]) + (w[11] + w[12])
    h2 = h2 + (((w[4] + w[9]) + (w[16] - w[1])) - (w[2] + w[19]))
    o2 = o2 + ((s2 + w[6]) - (w[0] + w[8]))
    h2o = h2o + (((w[2] + w[3]) + (w[5] + w[12])) + ((w[15] + w[18]) - w[20]))
    o = o + (((w[0] + w[3]) - (w[1] + w[7])) - ((w[6] + w[6]) + (w[11] + w[17])))
    ho2 = ho2 + (((s1 + w[8]) - s2) - (w[10] + w[13]))
    h2o2 = h2o2 + ((w[13] - s1) - (w[14] + w[15]))
    oh = ((oxygen - h2o) - o) - 2.0 * ((o2 + ho2) + h2o2)
    h = ((surplus - h2o) + (ho2 + o)) - 2.0 * (h2 - o2)
    return (h2, o2, h2o, h, o, oh, ho2, h2o2), p


def warmth(change, sums, k, heat):
    on_rows, on_reactions = heat_scalars(heat)
    rate = {r: on_reactions[r] * k[r] for r in on_reactions}
    rate[0] = rate[0] + rate.pop(8)
    rate[9] = rate[9] + rate.pop(10)
    rate[15] = rate[15] + rate.pop(16)
    terms = [rate[r] * total for r, total in sums.items()]
    terms += [weight * change[row] for weight, row in zip(on_rows, free_rows)]
    while len(terms) > 1:
        terms = [sum(terms[i + 1:i + 2], terms[i]) for i in range(0, len(terms), 2)]
    return terms[0]


def chemistry(u, counts, stride, log_rate, activation, heat, done, upto):
    k = prepare(u[9], stride, log_rate, activation)
    before = tuple(u[:8])
    kept = atoms(before)
    now, sums = before, None
    for turn in range(done, upto):
        now, p = substep(now, kept, k, None if turn == 0 else counts > float(turn))
        sums = p if sums is None else {r: sums[r] + p[r] for r in sums}
    change = [after - start for after, start in zip(now, before)]
    return change + [jnp.zeros_like(u[9]), warmth(change, sums, k, heat)]


def block_numbers(counts, i, row_index, ny):
    number = jnp.zeros(row_index.shape, jnp.int32)
    for j in range(ny):
        number = jnp.where(row_index == j, counts[i, j], number)
    return number.astype(jnp.float32)


def first_kernel(
    state, source, counts_in, diffusivity_in, log_rate_in, activation_in, heat_in,
    first_out, next_out,
    st, src, first, nxt, counts, diffusivity, log_rate, activation, heat, numbers,
    own_x, own_y, own_corners, fx, fy, hx1, hy1, corners, hx2, hy2,
    load_sem, store_sem, send_sem, recv_sem,
):
    rows, nx, ny, nz = st.shape
    x, size_x = lax.axis_index("gx"), lax.axis_size("gx")
    y, size_y = lax.axis_index("gy"), lax.axis_size("gy")
    x_up, x_down = lax.rem(x + 1, size_x), lax.rem(x + size_x - 1, size_x)
    y_up, y_down = lax.rem(y + 1, size_y), lax.rem(y + size_y - 1, size_y)
    sides = ((x_up, y), (x_down, y), (x, y_up), (x, y_down))
    diagonals = ((x_up, y_up), (x_up, y_down), (x_down, y_up), (x_down, y_down))
    barrier = pltpu.get_barrier_semaphore()
    for device in diagonals + sides:
        pl.semaphore_signal(barrier, inc=1, device_id=device, device_id_type=pl.DeviceIdType.MESH)
    pairs = (
        (state, st), (source, src), (diffusivity_in, diffusivity),
        (counts_in, counts), (log_rate_in, log_rate), (activation_in, activation), (heat_in, heat),
    )
    loads = [pltpu.make_async_copy(one, two, load_sem.at[n]) for n, (one, two) in enumerate(pairs)]
    for load in loads:
        load.start()

    def send(pieces, devices, base):
        copies = []
        for place, (piece, device) in enumerate(zip(pieces, devices)):
            copies.append(pltpu.make_async_remote_copy(
                src_ref=piece[0], dst_ref=piece[1],
                send_sem=send_sem.at[base + place], recv_sem=recv_sem.at[base + place],
                device_id=device, device_id_type=pl.DeviceIdType.MESH,
            ))
        for copy in copies[::-1]:
            copy.start()
        return copies

    def pack(k, carry):
        for i in range(nx):
            value = st[k, i]
            own_y[0, k, pl.ds(i, 1), :] = value[ny - 1:]
            own_y[1, k, pl.ds(i, 1), :] = value[:1]
            if i in (0, nx - 1):
                n = 0 if i == nx - 1 else 1
                own_x[n, k] = value
                own_corners[2 * n, k] = value[ny - 1:]
                own_corners[2 * n + 1, k] = value[:1]
        return carry

    loads[0].wait()
    lax.fori_loop(0, rows, pack, 0)
    pl.semaphore_wait(barrier, 8)
    state_copies = send((
        (own_x.at[0], hx1.at[0]), (own_x.at[1], hx1.at[1]), (own_y.at[0], hy1.at[0]), (own_y.at[1], hy1.at[1]),
    ), sides, 0)
    corner_copies = send(tuple((own_corners.at[n], corners.at[n]) for n in range(4)), diagonals, 4)

    row_index = lax.broadcasted_iota(jnp.int32, (ny, nz), 0)
    at_low, at_high = row_index == 0, row_index == ny - 1

    def inner_laplace(field, k, i):
        here = field[k, i]
        low = jnp.where(at_low, 0.0, pltpu.roll(here, 1, 0))
        high = jnp.where(at_high, 0.0, pltpu.roll(here, ny - 1, 0))
        beside = (low + high) + (pltpu.roll(here, 1, 1) + pltpu.roll(here, nz - 1, 1))
        if i > 0:
            beside = beside + field[k, i - 1]
        if i < nx - 1:
            beside = beside + field[k, i + 1]
        return beside - 6.0 * here

    def outer_laplace(halo_x, halo_y, k, i):
        low = jnp.where(at_low, halo_y[0, k, pl.ds(i, 1), :], 0.0)
        rest = jnp.where(at_high, halo_y[1, k, pl.ds(i, 1), :], low)
        if i == 0:
            rest = rest + halo_x[0, k]
        if i == nx - 1:
            rest = rest + halo_x[1, k]
        return rest

    def first_inner(k, carry):
        weight = time_step * diffusivity[k]
        for i in range(nx):
            value = (st[k, i] + time_step * src[k, i]) + weight * inner_laplace(st, k, i)
            first[k, i] = value
            fy[0, k, pl.ds(i, 1), :] = value[ny - 1:]
            fy[1, k, pl.ds(i, 1), :] = value[:1]
            if i == nx - 1:
                fx[0, k] = value
            if i == 0:
                fx[1, k] = value
        return carry

    for load in loads[1:3]:
        load.wait()
    lax.fori_loop(0, rows, first_inner, 0)
    first_copies = send((
        (fx.at[0], hx2.at[0]), (fx.at[1], hx2.at[1]), (fy.at[0], hy2.at[0]), (fy.at[1], hy2.at[1]),
    ), sides, 8)

    for load in loads[3:]:
        load.wait()
    for i in range(nx):
        numbers[i] = block_numbers(counts, i, row_index, ny)

    def early_group(i, carry):
        part = pl.ds(i * together, together)
        u = [st[s, part] for s in range(rows)]
        number = numbers[part]
        change = chemistry(u, number, time_step / number, log_rate, activation, heat, 0, most_steps)
        for s in range(rows):
            nxt[s, part] = 0.5 * (u[s] + change[s])
        return carry

    lax.fori_loop(0, nx // together, early_group, 0)

    def first_outer(k, carry):
        weight = time_step * diffusivity[k]
        for i in range(nx):
            first[k, i] = first[k, i] + weight * outer_laplace(hx1, hy1, k, i)
        return carry

    for copy in state_copies:
        copy.wait_recv()
    lax.fori_loop(0, rows, first_outer, 0)
    first_store = pltpu.make_async_copy(first, first_out, store_sem.at[0])
    first_store.start()

    def next_inner(k, carry):
        weight = (0.5 * time_step) * diffusivity[k]
        for i in range(nx):
            nxt[k, i] = (nxt[k, i] + 0.5 * first[k, i]) + weight * inner_laplace(first, k, i)
        return carry

    lax.fori_loop(0, rows, next_inner, 0)
    for copy in corner_copies + first_copies:
        copy.wait_recv()

    side_index = lax.broadcasted_iota(jnp.int32, (nx, nz), 0)

    def next_outer(k, carry):
        weight = time_step * diffusivity[k]
        corner = [corners[n, k] for n in range(4)]
        for n, plane in ((0, st[k, 0]), (1, st[k, nx - 1])):
            low = jnp.where(at_low, corner[2 * n], 0.0)
            rest = jnp.where(at_high, corner[2 * n + 1], low)
            hx2[n, k] = hx2[n, k] + weight * (plane + rest)
        for n in range(2):
            low = jnp.where(side_index == 0, corner[n], 0.0)
            rest = jnp.where(side_index == nx - 1, corner[2 + n], low)
            hy2[n, k] = hy2[n, k] + weight * (own_y[1 - n, k] + rest)
        for i in range(nx):
            nxt[k, i] = nxt[k, i] + (0.5 * weight) * outer_laplace(hx2, hy2, k, i)
        return carry

    half = rows // 2
    stores = [first_store]
    for n in range(2):
        lax.fori_loop(n * half, n * half + half, next_outer, 0)
        part = pl.ds(n * half, half)
        stores.append(pltpu.make_async_copy(nxt.at[part], next_out.at[part], store_sem.at[1 + n]))
        stores[-1].start()
    for copy in state_copies + corner_copies + first_copies:
        copy.wait_send()
    for store in stores:
        store.wait()


def second_kernel(
    first_in, next_in, counts_in, log_rate_in, activation_in, heat_in,
    next_out, late_out,
    first, nxt, late, counts, log_rate, activation, heat, small_sem, load_sem, next_sem, late_sem,
):
    rows, nx, ny, nz = first.shape
    groups = nx // together
    pairs = ((counts_in, counts), (log_rate_in, log_rate), (activation_in, activation), (heat_in, heat))
    small = [pltpu.make_async_copy(one, two, small_sem.at[n]) for n, (one, two) in enumerate(pairs)]

    def span(i):
        return pl.ds(i * together, together)

    def first_load(i):
        return pltpu.make_async_copy(first_in.at[:, span(i)], first.at[:, span(i)], load_sem.at[i])

    def late_store(i):
        return pltpu.make_async_copy(late.at[:, span(i)], late_out.at[:, span(i)], late_sem.at[i])

    def next_load(i):
        return pltpu.make_async_copy(next_in.at[:, span(i)], nxt.at[:, span(i)], next_sem.at[0, i])

    def next_store(i):
        return pltpu.make_async_copy(nxt.at[:, span(i)], next_out.at[:, span(i)], next_sem.at[1, i])

    for copy in small:
        copy.start()
    for i in range(groups):
        first_load(i).start()
        next_load(i).start()
    for copy in small:
        copy.wait()
    row_index = lax.broadcasted_iota(jnp.int32, (ny, nz), 0)

    def group(i, carry):
        last = counts[i * together, 0]
        for n in range(together):
            for j in range(ny):
                last = jnp.maximum(last, counts[i * together + n, j])
        number = jnp.stack([block_numbers(counts, i * together + n, row_index, ny) for n in range(together)])
        next_load(i).wait()
        next_store(i).start()
        first_load(i).wait()

        def run(upto):
            u = [first[s, span(i)] for s in range(rows)]
            change = chemistry(u, number, time_step / number, log_rate, activation, heat, 0, upto)
            for s in range(rows):
                late[s, span(i)] = change[s] * (1.0 / time_step)

        @pl.when(last <= late_steps)
        def _():
            run(late_steps)

        @pl.when(last > late_steps)
        def _():
            run(most_steps)

        late_store(i).start()
        return carry

    lax.fori_loop(0, groups, group, 0)
    for i in range(groups):
        next_store(i).wait()
        late_store(i).wait()


def local(state, source_in, counts, diffusivity, log_rate, activation, heat_release):
    rows, nx, ny, nz = state.shape
    whole = jax.ShapeDtypeStruct(state.shape, jnp.float32)
    field = pltpu.VMEM(state.shape, jnp.float32)
    outside = pl.BlockSpec(memory_space=pl.ANY)
    scalars = [pltpu.SMEM(a.shape, a.dtype) for a in (counts, log_rate, activation, heat_release)]
    halo_x = pltpu.VMEM((2, rows, ny, nz), jnp.float32)
    corner = pltpu.VMEM((4, rows, 1, nz), jnp.float32)
    halo_y = pltpu.VMEM((2, rows, nx, nz), jnp.float32)
    first, partial = pl.pallas_call(
        first_kernel,
        out_shape=(whole,) * 2,
        in_specs=[outside] * 7,
        out_specs=(outside,) * 2,
        scratch_shapes=[
            field, field, field, field,
            scalars[0], pltpu.SMEM(diffusivity.shape, jnp.float32), *scalars[1:],
            pltpu.VMEM((nx, ny, nz), jnp.float32),
            halo_x, halo_y, corner, halo_x, halo_y, halo_x, halo_y, corner, halo_x, halo_y,
            pltpu.SemaphoreType.DMA((7,)),
            pltpu.SemaphoreType.DMA((3,)),
            pltpu.SemaphoreType.DMA((12,)),
            pltpu.SemaphoreType.DMA((12,)),
        ],
        compiler_params=pltpu.CompilerParams(
            collective_id=0, has_side_effects=True, vmem_limit_bytes=60 * 1024 * 1024,
        ),
        name="sections",
    )(state, source_in, counts, diffusivity, log_rate, activation, heat_release)
    return pl.pallas_call(
        second_kernel,
        out_shape=(whole,) * 2,
        in_specs=[outside] * 6,
        out_specs=(outside,) * 2,
        scratch_shapes=[
            field, field, field, *scalars,
            pltpu.SemaphoreType.DMA((4,)),
            pltpu.SemaphoreType.DMA((nx // together,)),
            pltpu.SemaphoreType.DMA((2, nx // together)),
            pltpu.SemaphoreType.DMA((nx // together,)),
        ],
        compiler_params=pltpu.CompilerParams(vmem_limit_bytes=60 * 1024 * 1024),
        name="finish",
    )(first, partial, counts, log_rate, activation, heat_release)


def solution(mesh):
    grid = P(None, "gx", "gy", None)
    return jax.shard_map(
        local,
        mesh=mesh,
        in_specs=(grid, grid, P("gx", "gy"), P(), P(), P(), P()),
        out_specs=(grid, grid),
        check_vma=False,
    )
```
